256 devices in a mesh: table: 64 (over z, y, core), batch: 4 (over x).
Axes of the slice: x: 4, y: 4, z: 8, core: 2. Of those that a mesh axis runs over, the one named last changes fastest.
Arguments:
- embedding_table: bfloat16 [524288, 128], P('table'), may hold values from -6 to 6
- request_rows: int32 [256, 2048], P(('table', 'batch')), may hold values from -1 to 8191, as said below
- node_slots: int32 [262144, 2], P(('table', 'batch')), may hold values from 0 to 2047, as said below
- neighbours: int32 [262144, 8], P(('table', 'batch')), may hold values from 0 to 1023
- kept_edges: int32 [2, 262144, 8], P(None, ('table', 'batch')), may hold values 0 or 1
- weight_one: bfloat16 [128, 256], replicated, may hold values from -0.5 to 0.5
- weight_two: bfloat16 [256, 256], replicated, may hold values from -0.375 to 0.375
- proj_first: bfloat16 [256, 256], replicated, may hold values from -0.375 to 0.375
- proj_second: bfloat16 [256, 256], replicated, may hold values from -0.375 to 0.375
Outputs:
- table_grad: float32 [524288, 128], P(('table', 'batch'))
The draws below stay inside these ranges and needn't reach their ends.
Inputs may be any that keep to these rules, and one draw needn't show every extreme that they name: `request_rows`: in each device's row, slab p (slots p * 32 to p * 32 + 31) lists rows of table index p, its used slots first and -1 in the rest. Every device fills some slab completely, and some table index receives a full slab from every device. `node_slots`: each entry names a used slot of its own device's request list, and every used slot is named by some node of that device.
All inputs are finite; a program needn't handle non-finite values. No bound on the sum of `kept_edges` on one device may be relied on, other than what follows from the above.
Results may differ from the reference program's by a relative error of at most 0.0095.
The reference program's roundings to bfloat16 on the way (of `layer_in`, `hidden`, `seed_in`, `inner`, `projected`, `unit_keys`, `forward_w` and `backward_w`) count: a program that leaves them out, or rounds other values in their place, can miss the bound.
Values may be sent and summed in bfloat16 or wider, within the bound.
No kernel may reach another device: no remote copies, remote signals or barrier semaphores. Data moves between devices by JAX's collectives and lax.ppermute only.
A program may use at most 128 MiB of HBM per device.

```python
import jax
import jax.numpy as jnp
from jax import lax

D = 128
F = 256
H = 2
DEG = 8
SEED_DEV = 256
ROW_DEV = 8192
NODE_DEV = 1024
CAP = 32
NODES = 262144
GROUP = 1024
ROWS = 524288
N_TABLE = 64
N_BATCH = 4


def shared_requests(key):
    device_count = N_TABLE * N_BATCH
    base_counts = jax.random.randint(jax.random.fold_in(key, 11), (device_count, N_TABLE), CAP // 4, CAP // 2 + 1)
    hottest = jax.random.randint(jax.random.fold_in(key, 12), (), 0, N_TABLE)
    second_full = jax.random.randint(jax.random.fold_in(key, 13), (device_count, 1), 0, N_TABLE)
    owners = jnp.arange(N_TABLE, dtype=jnp.int32)[None, :]
    counts = jnp.where((owners == hottest) | (owners == second_full), CAP, base_counts).astype(jnp.int32)
    row_starts = jax.random.randint(jax.random.fold_in(key, 14), (device_count, N_TABLE, 1), 0, ROW_DEV)
    strides = 2 * jax.random.randint(jax.random.fold_in(key, 15), (device_count, N_TABLE, 1), 0, ROW_DEV // 2) + 1
    positions = jnp.arange(CAP, dtype=jnp.int32)[None, None, :]
    row_offsets = (row_starts + positions * strides) % ROW_DEV
    requests = jnp.where(positions < counts[:, :, None], row_offsets, -1)
    return (counts, requests.reshape(device_count, N_TABLE * CAP).astype(jnp.int32))


def draw_request_rows(key, part):
    counts, requests = shared_requests(key)
    return requests


def draw_node_slots(key, part):
    counts, requests = shared_requests(key)
    key = jax.random.fold_in(key, 5)
    device_count = N_TABLE * N_BATCH
    wanted = NODE_DEV * H
    device_keys = jax.random.split(key, device_count)
    orders = jax.vmap(lambda single: jax.random.permutation(single, wanted))(device_keys)
    used = jnp.sum(counts, axis=1, keepdims=True)
    picks = orders % used
    ends = jnp.cumsum(counts, axis=1)
    owner = jax.vmap(lambda edge, pick: jnp.searchsorted(edge, pick, side='right'))(ends, picks).astype(jnp.int32)
    firsts = ends - counts
    offset = picks - jnp.take_along_axis(firsts, owner, axis=1)
    return (owner * CAP + offset).reshape(device_count * NODE_DEV, H).astype(jnp.int32)


def touch_ends(drawn, key, least, largest):
    longest = drawn.shape.index(max(drawn.shape))
    spots = []
    for shift in (0, 1):
        where = [jax.random.randint(jax.random.fold_in(key, axis), (), 0, length) for axis, length in enumerate(drawn.shape)]
        where[longest] = (where[longest] + shift) % drawn.shape[longest]
        spots.append(tuple(where))
    return drawn.at[spots[0]].set(least).at[spots[1]].set(largest)


def block_scale(own_key, extent, cuts, low, largest):
    level, own = 1.0, jax.random.fold_in(own_key, 6)
    for axis_at, blocks in cuts:
        draws = jnp.exp(jax.random.uniform(jax.random.fold_in(own, axis_at), (blocks,), jnp.float32, low / len(cuts), largest / len(cuts)))
        level = level * jnp.repeat(draws, extent[axis_at] // blocks).reshape([-1 if axis == axis_at else 1 for axis in range(len(extent))])
    return level


def centred(rng, dims, scale, most, shards=(), kind=jnp.bfloat16):
    values = jax.random.normal(rng, dims, jnp.float32) * scale
    if len(shards) > 0:
        values = block_scale(rng, dims, shards, -0.22, 0.18) * values
    return jnp.clip(values, min=-most, max=most).astype(kind)


def setup_inputs(seed: int = 0) -> dict:
    key_of = jax.random.split(jax.random.key(seed), 10)
    embedding_table = centred(key_of[0], (ROWS, D), 1.0, 6.0, ((0, 64),))
    request_rows = draw_request_rows(jax.random.fold_in(key_of[9], 71), 0)
    node_slots = draw_node_slots(jax.random.fold_in(key_of[9], 71), 0)
    neighbours = touch_ends(jax.random.randint(key_of[3], (NODES, DEG), 0, NODE_DEV), jax.random.fold_in(key_of[3], 1), 0, NODE_DEV - 1).astype(jnp.int32)
    kept_edges = touch_ends((jax.random.randint(key_of[4], (2, NODES, DEG), 0, 5) < 4).astype(jnp.int32), jax.random.fold_in(key_of[4], 1), 0, 1)
    weight_one = centred(key_of[5], (D, F), D ** -0.5, 0.5)
    weight_two = centred(key_of[6], (F, F), F ** -0.5, 0.375)
    proj_first = centred(key_of[7], (F, F), F ** -0.5, 0.375)
    proj_second = centred(key_of[8], (F, F), F ** -0.5, 0.375)
    return dict(embedding_table=embedding_table, request_rows=request_rows, node_slots=node_slots, neighbours=neighbours, kept_edges=kept_edges, weight_one=weight_one, weight_two=weight_two, proj_first=proj_first, proj_second=proj_second)


TEMPER = 0.25
EPSILON = 1e-06

def aggregate(values, neighbours, kept):
    weights = kept.astype(jnp.float32)
    gathered = values[neighbours]
    summed = values[:neighbours.shape[0]] + lax.optimization_barrier(jnp.sum(weights[:, :, None] * gathered, axis=1))
    return summed / (1.0 + lax.optimization_barrier(jnp.sum(weights, axis=1)))[:, None]

def encode(features, neighbours, kept_edges, weight_one, weight_two, proj_first, proj_second):
    outputs = []
    for which_view in range(2):
        layer_in = aggregate(features, neighbours, kept_edges[which_view]).astype(jnp.bfloat16)
        hidden = jax.nn.relu(jnp.dot(layer_in, weight_one, preferred_element_type=jnp.float32)).astype(jnp.bfloat16)
        seed_in = aggregate(hidden.astype(jnp.float32), neighbours[:SEED_DEV], kept_edges[which_view, :SEED_DEV]).astype(jnp.bfloat16)
        inner = jax.nn.relu(jnp.dot(seed_in, weight_two, preferred_element_type=jnp.float32)).astype(jnp.bfloat16)
        projected = jax.nn.elu(jnp.dot(inner, proj_first, preferred_element_type=jnp.float32)).astype(jnp.bfloat16)
        outputs.append(jnp.dot(projected, proj_second, preferred_element_type=jnp.float32))
    return jnp.stack(outputs)

def normalize(raw):
    return raw / jnp.sqrt(lax.optimization_barrier(jnp.sum(raw * raw, axis=-1, keepdims=True)) + EPSILON)

def contrast(keys):
    key_count = keys.shape[0]
    half_count = key_count // 2
    scores = jnp.dot(keys, keys.T, preferred_element_type=jnp.float32) / TEMPER
    same = jnp.arange(key_count, dtype=jnp.int32)[:, None] == jnp.arange(key_count, dtype=jnp.int32)[None, :]
    exponent = jnp.where(same, 0.0, jnp.exp(scores))
    totals = lax.optimization_barrier(jnp.sum(exponent, axis=1))
    probs = exponent / totals[:, None]
    forward_w = probs.astype(jnp.bfloat16)
    backward_w = probs.T.astype(jnp.bfloat16)
    partner = jnp.roll(keys, half_count, axis=0).astype(jnp.float32)
    direct = jnp.dot(forward_w, keys, preferred_element_type=jnp.float32)
    reverse = jnp.dot(backward_w, keys, preferred_element_type=jnp.float32)
    return (direct + reverse - 2.0 * partner) / TEMPER

def reference(embedding_table, request_rows, node_slots, neighbours, kept_edges, weight_one, weight_two, proj_first, proj_second):
    device_count = N_TABLE * N_BATCH
    block_of = (jnp.arange(NODES, dtype=jnp.int32) // NODE_DEV)[:, None]
    row_index = node_slots // CAP * ROW_DEV + request_rows[block_of, node_slots]
    features = lax.optimization_barrier(jnp.sum(embedding_table[row_index].astype(jnp.float32), axis=1))
    feature_blocks = features.reshape(device_count, NODE_DEV, D)
    near_blocks = neighbours.reshape(device_count, NODE_DEV, DEG)
    kept_blocks = jnp.transpose(kept_edges.reshape(2, device_count, NODE_DEV, DEG), (1, 0, 2, 3))

    def forward_block(items):
        return encode(items[0], items[1], items[2], weight_one, weight_two, proj_first, proj_second)
    raw = lax.map(forward_block, (feature_blocks, near_blocks, kept_blocks))
    unit_keys = normalize(raw).astype(jnp.bfloat16)
    grouped = jnp.transpose(unit_keys.reshape(N_TABLE, N_BATCH, 2, SEED_DEV, F), (0, 2, 1, 3, 4)).reshape(N_TABLE, 2 * GROUP, F)
    key_grads = lax.map(contrast, grouped)
    key_grads = jnp.transpose(key_grads.reshape(N_TABLE, 2, N_BATCH, SEED_DEV, F), (0, 2, 1, 3, 4)).reshape(device_count, 2, SEED_DEV, F)

    def backward_block(items):
        values, near, kept, raw_block, cotangent = items

        def forward(inputs):
            return encode(inputs, near, kept, weight_one, weight_two, proj_first, proj_second)
        unused_raw, encode_back = jax.vjp(forward, values)
        unused_unit, norm_back = jax.vjp(normalize, raw_block)
        return encode_back(norm_back(cotangent)[0])[0]
    feature_grads = lax.map(backward_block, (feature_blocks, near_blocks, kept_blocks, raw, key_grads)).reshape(NODES, D)
    spread = jnp.broadcast_to(feature_grads[:, None, :], (NODES, H, D)).reshape(NODES * H, D)
    return jax.ops.segment_sum(spread, row_index.reshape(-1), num_segments=ROWS)
```

```python
import functools

import jax
import jax.numpy as jnp
from jax import lax
from jax.experimental import pallas as pl
from jax.experimental.pallas import tpu as pltpu
from jax.sharding import PartitionSpec as P

SEED_DEV = 256
TEMPER = 0.25
EPSILON = 1e-06
F32 = jnp.float32
BF16 = jnp.bfloat16
VMEM_BYTES = 48 * 1024 * 1024
VMEM = pl.BlockSpec(memory_space=pltpu.VMEM)


def nn(left, right):
    return lax.dot_general(left, right, (((1,), (0,)), ((), ())), preferred_element_type=F32)


def nt(left, right):
    return lax.dot_general(left, right, (((1,), (1,)), ((), ())), preferred_element_type=F32)


def tn(left, right):
    return lax.dot_general(left, right, (((0,), (0,)), ((), ())), preferred_element_type=F32)


def split(values):
    high = values.astype(BF16)
    low = (values - high.astype(F32)).astype(BF16)
    return jnp.concatenate([high, low], axis=0)


def call(kernel, outs, args, flops, moved, aliases=None):
    return pl.pallas_call(
        kernel,
        out_shape=outs,
        in_specs=[VMEM] * len(args),
        out_specs=[VMEM] * len(outs),
        input_output_aliases=aliases or {},
        compiler_params=pltpu.CompilerParams(vmem_limit_bytes=VMEM_BYTES),
        cost_estimate=pl.CostEstimate(flops=flops, bytes_accessed=moved, transcendentals=0),
    )(*args)


def edges_kernel(near_ref, counts_ref):
    views, slots, nodes = near_ref.shape
    rows = 32

    def step(block, carry):
        start = pl.multiple_of(block * rows, rows)
        ids = lax.broadcasted_iota(jnp.int32, (rows, nodes), 0) + start
        own = (ids == lax.broadcasted_iota(jnp.int32, (rows, nodes), 1)).astype(F32)
        for view in range(views):
            total = own
            for slot in range(slots):
                near = near_ref[view, slot : slot + 1, :]
                total = total + jnp.where(near == ids, 1.0, 0.0)
            counts_ref[view, pl.ds(start, rows), :] = total.astype(BF16)
        return carry

    lax.fori_loop(0, nodes // rows, step, 0)


def slots_kernel(slot_ref, counts_ref):
    hashes, nodes = slot_ref.shape
    rows = 32

    def step(block, carry):
        start = pl.multiple_of(block * rows, rows)
        ids = lax.broadcasted_iota(jnp.int32, (rows, nodes), 0) + start
        total = jnp.where(slot_ref[0:1, :] == ids, 1.0, 0.0)
        for which in range(1, hashes):
            total = total + jnp.where(slot_ref[which : which + 1, :] == ids, 1.0, 0.0)
        counts_ref[pl.ds(start, rows), :] = total.astype(BF16)
        return carry

    lax.fori_loop(0, counts_ref.shape[0] // rows, step, 0)


def forward_kernel(
    rows_ref, slots_ref, edges_ref, degree_ref, one_ref, two_ref, first_ref, second_ref,
    keys_ref, raw_ref, hidden_ref, inner_ref, slope_ref,
):
    seeds = SEED_DEV
    width = rows_ref.shape[1]
    features = split(tn(rows_ref[...], slots_ref[...]))
    for view in range(2):
        edges = edges_ref[view]
        degree = degree_ref[view : view + 1, :]
        summed = nn(features, edges)
        layer_in = ((summed[:width] + summed[width:]) / degree).astype(BF16)
        hidden = jnp.maximum(tn(one_ref[...], layer_in), 0.0).astype(BF16)
        hidden_ref[view] = hidden
        seed_in = (nn(hidden, edges[:, :seeds]) / degree[:, :seeds]).astype(BF16)
        inner = jnp.maximum(tn(two_ref[...], seed_in), 0.0).astype(BF16)
        before = tn(first_ref[...], inner)
        grown = jnp.exp(jnp.minimum(before, 0.0))
        near_zero = before * (1.0 + before * (0.5 + before * (1.0 / 6.0)))
        below = jnp.where(before > -0.01, near_zero, grown - 1.0)
        projected = jnp.where(before > 0.0, before, below).astype(BF16)
        raw = tn(second_ref[...], projected)
        scale = lax.rsqrt(jnp.sum(raw * raw, axis=0, keepdims=True) + EPSILON)
        span = slice(view * seeds, (view + 1) * seeds)
        keys_ref[:, span] = (raw * scale).astype(BF16)
        raw_ref[:, span] = raw
        inner_ref[:, span] = inner
        slope_ref[:, span] = jnp.where(before > 0.0, 1.0, grown)


def backward_kernel(
    key0_ref, key1_ref, key2_ref, key3_ref, raw_ref, hidden_ref, inner_ref, slope_ref,
    slots_ref, edges_ref, degree_ref, one_ref, two_ref, first_ref, second_ref,
    grads_ref, expo_ref,
):
    seeds = SEED_DEV
    keys_t = [ref[...] for ref in (key0_ref, key1_ref, key2_ref, key3_ref)]
    count = keys_t[0].shape[1]
    totals_own = jnp.zeros((1, count), F32)
    totals = []
    same = lax.broadcasted_iota(jnp.int32, (count, count), 0) == lax.broadcasted_iota(
        jnp.int32, (count, count), 1
    )
    for block in range(4):
        keys = keys_t[block].T
        total = jnp.zeros((count, 1), F32)
        for other in range(4):
            expo = jnp.exp(nn(keys, keys_t[other]) * (1.0 / TEMPER))
            if other == block:
                expo = jnp.where(same, 0.0, expo)
            total = total + jnp.sum(expo, axis=1, keepdims=True)
            if other == 0:
                expo_ref[block * count : (block + 1) * count, :] = expo
                totals_own = totals_own + jnp.sum(expo, axis=0, keepdims=True)
        totals.append(total)
    own_inverse = 1.0 / totals_own
    pulled = jnp.zeros((keys_t[0].shape[0], count), F32)
    for block in range(4):
        expo = expo_ref[block * count : (block + 1) * count, :]
        weights = (expo * (own_inverse + 1.0 / totals[block])).astype(BF16)
        pulled = pulled + nn(keys_t[block], weights)
    feature_grads = None
    for view in range(2):
        span = slice(view * seeds, (view + 1) * seeds)
        other = slice((1 - view) * seeds, (2 - view) * seeds)
        partner = key0_ref[:, other].astype(F32)
        key_grads = (pulled[:, span] - 2.0 * partner) * (1.0 / TEMPER)
        raw = raw_ref[:, span]
        scale = lax.rsqrt(jnp.sum(raw * raw, axis=0, keepdims=True) + EPSILON)
        along = jnp.sum(raw * key_grads, axis=0, keepdims=True) * (scale * scale)
        raw_grads = ((key_grads - raw * along) * scale).astype(BF16)
        grads = nn(second_ref[...], raw_grads).astype(BF16).astype(F32)
        grads = (grads * slope_ref[:, span]).astype(BF16)
        grads = nn(first_ref[...], grads).astype(BF16)
        grads = jnp.where(inner_ref[:, span] > 0, grads, jnp.zeros_like(grads))
        grads = nn(two_ref[...], grads).astype(BF16).astype(F32)
        degree = degree_ref[view : view + 1, :]
        wide = grads.shape[0]
        grads = nt(split(grads / degree[:, :seeds]), edges_ref[view, :, :seeds])
        grads = (grads[:wide] + grads[wide:]).astype(BF16)
        grads = jnp.where(hidden_ref[view] > 0, grads, jnp.zeros_like(grads))
        grads = nn(one_ref[...], grads).astype(BF16).astype(F32)
        grads = nt(split(grads / degree), edges_ref[view])
        feature_grads = grads if feature_grads is None else feature_grads + grads
    width = feature_grads.shape[0] // 2
    feature_grads = split(feature_grads[:width] + feature_grads[width:])
    slot_grads = nt(slots_ref[...], feature_grads)
    grads_ref[...] = (slot_grads[:, :width] + slot_grads[:, width:]).astype(BF16)


def scatter_kernel(row_ref, lane_ref, grads_ref, *rest, first):
    out_ref = rest[-1]
    count, width = grads_ref.shape
    parts = 4
    rows = out_ref.shape[0] // parts
    low = row_ref[...] & (rows - 1)
    hit = low == lax.broadcasted_iota(jnp.int32, (rows, count), 0)
    pick = jnp.where(hit, 1.0, 0.0).astype(BF16)
    grads = grads_ref[...].astype(F32)
    part_of = lane_ref[...]
    for part in range(parts):
        chosen = jnp.where(part_of == part, grads, 0.0).astype(BF16)
        added = nn(pick, chosen)
        span = slice(part * rows, (part + 1) * rows)
        if not first:
            added = added + rest[0][span, :]
        out_ref[span, :] = added


def body(
    embedding_table,
    request_rows,
    node_slots,
    neighbours,
    kept_edges,
    weight_one,
    weight_two,
    proj_first,
    proj_second,
):
    table_count = lax.axis_size("table")
    batch_count = lax.axis_size("batch")
    shard_rows, width = embedding_table.shape
    nodes = neighbours.shape[0]
    seeds = SEED_DEV
    requests = request_rows.reshape(table_count, -1)
    slot_count = requests.size

    def turn(value, by):
        return lax.ppermute(
            value, "batch", [(source, (source + by) % batch_count) for source in range(batch_count)]
        )

    def exchange(value):
        return [value] + [turn(value, by) for by in range(1, batch_count)]

    received = lax.all_to_all(requests, "table", split_axis=0, concat_axis=0, tiled=True)
    fetched = embedding_table[jnp.maximum(received, 0)]
    arrived = lax.all_to_all(fetched, "table", split_axis=0, concat_axis=0, tiled=True)
    rows = arrived.reshape(slot_count, width)

    near = jnp.where(kept_edges > 0, neighbours[None], -1).transpose(0, 2, 1)
    degree = 1.0 + jnp.sum(kept_edges, axis=2).astype(F32)
    (edges,) = call(
        edges_kernel,
        [jax.ShapeDtypeStruct((2, nodes, nodes), BF16)],
        [near],
        flops=60_000_000,
        moved=4 * nodes * nodes,
    )
    (slots,) = call(
        slots_kernel,
        [jax.ShapeDtypeStruct((slot_count, nodes), BF16)],
        [node_slots.T],
        flops=10_000_000,
        moved=2 * nodes * slot_count,
    )
    wide = weight_one.shape[1]
    keys, raw, hidden, inner, slope = call(
        forward_kernel,
        [
            jax.ShapeDtypeStruct((wide, 2 * seeds), BF16),
            jax.ShapeDtypeStruct((wide, 2 * seeds), F32),
            jax.ShapeDtypeStruct((2, wide, nodes), BF16),
            jax.ShapeDtypeStruct((wide, 2 * seeds), BF16),
            jax.ShapeDtypeStruct((wide, 2 * seeds), F32),
        ],
        [rows, slots, edges, degree, weight_one, weight_two, proj_first, proj_second],
        flops=2_400_000_000,
        moved=10_000_000,
    )
    group_keys = exchange(keys)
    grads = pl.pallas_call(
        backward_kernel,
        out_shape=jax.ShapeDtypeStruct((slot_count, width), BF16),
        in_specs=[VMEM] * 15,
        out_specs=VMEM,
        scratch_shapes=[pltpu.VMEM((2 * seeds * batch_count, 2 * seeds), F32)],
        compiler_params=pltpu.CompilerParams(vmem_limit_bytes=VMEM_BYTES),
        cost_estimate=pl.CostEstimate(
            flops=8_000_000_000, bytes_accessed=12_000_000, transcendentals=4_000_000
        ),
    )(
        *group_keys, raw, hidden, inner, slope, slots, edges, degree,
        weight_one, weight_two, proj_first, proj_second,
    )
    returned = lax.all_to_all(
        grads.reshape(table_count, -1, width), "table", split_axis=0, concat_axis=0, tiled=True
    ).reshape(slot_count, width)

    out_rows = shard_rows // batch_count
    part_rows = out_rows // 4
    offset = lax.axis_index("batch") * out_rows
    owned = exchange(received)
    parts = exchange(returned)
    total = None
    for index, piece in zip(owned, parts):
        index = index.reshape(-1) - offset
        lanes = jnp.broadcast_to((index // part_rows)[:, None], (slot_count, width))
        args = [index[None, :], lanes, piece] + ([] if total is None else [total])
        (total,) = call(
            functools.partial(scatter_kernel, first=total is None),
            [jax.ShapeDtypeStruct((out_rows, width), F32)],
            args,
            flops=1_000_000_000,
            moved=4_000_000,
            aliases={} if total is None else {3: 0},
        )
    return total


def solution(mesh):
    in_specs = (
        P("table", None),
        P(("table", "batch"), None),
        P(("table", "batch"), None),
        P(("table", "batch"), None),
        P(None, ("table", "batch"), None),
        P(),
        P(),
        P(),
        P(),
    )
    out_specs = P(("table", "batch"), None)
    return jax.shard_map(body, mesh=mesh, in_specs=in_specs, out_specs=out_specs, check_vma=False)
```

```python
import functools

import jax
import jax.numpy as jnp
from jax import lax
from jax.experimental import pallas as pl
from jax.experimental.pallas import tpu as pltpu
from jax.sharding import PartitionSpec as P

SEED_DEV = 256
TEMPER = 0.25
EPSILON = 1e-06
F32 = jnp.float32
BF16 = jnp.bfloat16
VMEM = pl.BlockSpec(memory_space=pltpu.VMEM)
HBM = pl.BlockSpec(memory_space=pltpu.HBM)


def nn(left, right):
    return lax.dot_general(left, right, (((1,), (0,)), ((), ())), preferred_element_type=F32)


def nt(left, right):
    return lax.dot_general(left, right, (((1,), (1,)), ((), ())), preferred_element_type=F32)


def tn(left, right):
    return lax.dot_general(left, right, (((0,), (0,)), ((), ())), preferred_element_type=F32)


def split(values):
    high = values.astype(BF16)
    low = (values - high.astype(F32)).astype(BF16)
    return jnp.concatenate([high, low], axis=0)


def call(kernel, outs, args, flops, moved, mib, scratch=(), far=(), far_outs=()):
    return pl.pallas_call(
        kernel,
        out_shape=outs,
        in_specs=[
            HBM if place in far else VMEM for place in range(len(args))
        ],
        out_specs=[HBM if place in far_outs else VMEM for place in range(len(outs))],
        scratch_shapes=list(scratch),
        compiler_params=pltpu.CompilerParams(vmem_limit_bytes=mib * 1024 * 1024),
        cost_estimate=pl.CostEstimate(flops=flops, bytes_accessed=moved, transcendentals=0),
    )(*args)


TILE, LANES, ROWS = 16, 128, 64


def spread(row, kind):
    return jnp.broadcast_to(row, (TILE, LANES)).astype(kind)


def places(axis):
    return lax.broadcasted_iota(jnp.int32, (TILE, LANES), axis)


def edges_kernel(near_ref, kept_ref, edges_far, edges_ref, sem):
    views, degree, nodes = kept_ref.shape
    none = jnp.zeros((), BF16)
    copies = []
    for part in range(nodes // LANES):
        span = slice(part * LANES, (part + 1) * LANES)
        nears = [spread(near_ref[slot : slot + 1, span], jnp.int16) for slot in range(degree)]
        kept = [
            [spread(kept_ref[view, slot : slot + 1, span], BF16) for slot in range(degree)]
            for view in range(views)
        ]

        def step(block, carry):
            for tile in range(ROWS // TILE):
                start = pl.multiple_of(block * ROWS + tile * TILE, TILE)
                ids = places(0) + start
                own = jnp.where(ids == places(1) + part * LANES, 1.0, 0.0).astype(BF16)
                ids = ids.astype(jnp.int16)
                totals = [own] * views
                for slot in range(degree):
                    hit = nears[slot] == ids
                    for view in range(views):
                        totals[view] = totals[view] + jnp.where(hit, kept[view][slot], none)
                for view in range(views):
                    edges_ref[view, pl.ds(start, TILE), span] = totals[view]
            return carry

        lax.fori_loop(0, nodes // ROWS, step, 0)
        copies.append(
            pltpu.make_async_copy(edges_ref.at[:, :, span], edges_far.at[:, :, span], sem.at[part])
        )
        copies[-1].start()
    for copy in copies:
        copy.wait()


def slots_kernel(slot_ref, slots_far, slots_ref, sem):
    hashes, nodes = slot_ref.shape
    one, none = jnp.ones((), BF16), jnp.zeros((), BF16)
    copies = []
    for part in range(nodes // LANES):
        span = slice(part * LANES, (part + 1) * LANES)
        named = [spread(slot_ref[which : which + 1, span], jnp.int16) for which in range(hashes)]

        def step(block, carry):
            for tile in range(ROWS // TILE):
                start = pl.multiple_of(block * ROWS + tile * TILE, TILE)
                ids = (places(0) + start).astype(jnp.int16)
                total = jnp.where(named[0] == ids, one, none)
                for which in range(1, hashes):
                    total = total + jnp.where(named[which] == ids, one, none)
                slots_ref[pl.ds(start, TILE), span] = total
            return carry

        lax.fori_loop(0, slots_ref.shape[0] // ROWS, step, 0)
        copies.append(
            pltpu.make_async_copy(slots_ref.at[:, span], slots_far.at[:, span], sem.at[part])
        )
        copies[-1].start()
    for copy in copies:
        copy.wait()


def slot_parts(source, target, sems):
    count = sems.shape[0]
    part = target.shape[0] // count
    spans = [pl.ds(place * part, part) for place in range(count)]
    return [
        pltpu.make_async_copy(source.at[span], target.at[span], sems.at[place])
        for place, span in enumerate(spans)
    ]


def forward_kernel(
    rows_ref, slots_ref, edges_ref, degree_ref, one_ref, two_ref, first_ref, second_ref,
    keys_ref, raw_ref, hidden_ref, inner_ref, slope_ref,
):
    seeds = SEED_DEV
    width = rows_ref.shape[1]
    features = split(tn(rows_ref[...], slots_ref[...]))
    for view in range(2):
        edges = edges_ref[view]
        degree = degree_ref[view : view + 1, :]
        summed = nn(features, edges)
        layer_in = ((summed[:width] + summed[width:]) / degree).astype(BF16)
        hidden = jnp.maximum(tn(one_ref[...], layer_in), 0.0).astype(BF16)
        hidden_ref[view] = hidden
        seed_in = (nn(hidden, edges[:, :seeds]) / degree[:, :seeds]).astype(BF16)
        inner = jnp.maximum(tn(two_ref[...], seed_in), 0.0).astype(BF16)
        before = tn(first_ref[...], inner)
        grown = jnp.exp(jnp.minimum(before, 0.0))
        near_zero = before * (1.0 + before * (0.5 + before * (1.0 / 6.0)))
        below = jnp.where(before > -0.01, near_zero, grown - 1.0)
        projected = jnp.where(before > 0.0, before, below).astype(BF16)
        raw = tn(second_ref[...], projected)
        scale = lax.rsqrt(jnp.sum(raw * raw, axis=0, keepdims=True) + EPSILON)
        span = slice(view * seeds, (view + 1) * seeds)
        keys_ref[:, span] = (raw * scale).astype(BF16)
        raw_ref[:, span] = raw
        inner_ref[:, span] = inner
        slope_ref[:, span] = jnp.where(before > 0.0, 1.0, grown)


def flip(row):
    return jnp.broadcast_to(row, (128, row.shape[1])).T[:, :1]


def pair_expo(left, right_t, same=None):
    expo = jnp.exp(nn(left, right_t) * (1.0 / TEMPER))
    return expo if same is None else jnp.where(same, 0.0, expo)


def diagonal(count):
    down = lax.broadcasted_iota(jnp.int32, (count, count), 0)
    return down == lax.broadcasted_iota(jnp.int32, (count, count), 1)


def down_sum(expo):
    return jnp.sum(expo, axis=0, keepdims=True)


def across_sum(expo):
    return jnp.sum(expo, axis=1, keepdims=True)


def early_kernel(key0_ref, key1_ref, key3_ref, expo_ref, total0_ref, totals_ref):
    own, ahead, behind = key0_ref[...], key1_ref[...], key3_ref[...]
    count = own.shape[1]
    same = diagonal(count)
    expo = pair_expo(own.T, own, same)
    expo_ref[:count, :] = expo
    total0 = down_sum(expo)
    left = ahead.T
    expo = pair_expo(left, own)
    expo_ref[count : 2 * count, :] = expo
    total0 = total0 + down_sum(expo)
    total1 = across_sum(expo) + across_sum(pair_expo(left, ahead, same))
    left = behind.T
    expo = pair_expo(left, own)
    expo_ref[2 * count :, :] = expo
    total0 = total0 + down_sum(expo)
    total3 = across_sum(expo) + across_sum(pair_expo(left, behind, same))
    expo = pair_expo(left, ahead)
    total3 = total3 + across_sum(expo)
    total1 = total1 + flip(down_sum(expo))
    total0_ref[...] = total0
    totals_ref[:count, :] = total1
    totals_ref[count:, :] = total3


def backward_kernel(
    key0_ref, key1_ref, key3_ref, key2_ref, expo_ref, total0_ref, totals_ref,
    raw_ref, hidden_ref, inner_ref, slope_ref,
    slots_ref, edges_ref, degree_ref, one_ref, two_ref, first_ref, second_ref,
    grads_ref,
):
    seeds = SEED_DEV
    far = key2_ref[...]
    count = far.shape[1]
    left = far.T
    last = pair_expo(left, key0_ref[...])
    total0 = total0_ref[...] + down_sum(last)
    total2 = across_sum(last) + across_sum(pair_expo(left, far, diagonal(count)))
    expo = pair_expo(left, key1_ref[...])
    total2 = total2 + across_sum(expo)
    total1 = totals_ref[:count, :] + flip(down_sum(expo))
    expo = pair_expo(left, key3_ref[...])
    total2 = total2 + across_sum(expo)
    total3 = totals_ref[count:, :] + flip(down_sum(expo))
    own_inverse = 1.0 / total0
    pulled = jnp.zeros(far.shape, F32)
    blocks = (
        (key0_ref, expo_ref[:count, :], flip(total0)),
        (key1_ref, expo_ref[count : 2 * count, :], total1),
        (key3_ref, expo_ref[2 * count :, :], total3),
        (key2_ref, last, total2),
    )
    for key_ref, expo, total in blocks:
        weights = (expo * (own_inverse + 1.0 / total)).astype(BF16)
        pulled = pulled + nn(key_ref[...], weights)
    feature_grads = None
    for view in range(2):
        span = slice(view * seeds, (view + 1) * seeds)
        other = slice((1 - view) * seeds, (2 - view) * seeds)
        partner = key0_ref[:, other].astype(F32)
        key_grads = (pulled[:, span] - 2.0 * partner) * (1.0 / TEMPER)
        raw = raw_ref[:, span]
        scale = lax.rsqrt(jnp.sum(raw * raw, axis=0, keepdims=True) + EPSILON)
        along = jnp.sum(raw * key_grads, axis=0, keepdims=True) * (scale * scale)
        raw_grads = ((key_grads - raw * along) * scale).astype(BF16)
        grads = nn(second_ref[...], raw_grads).astype(BF16).astype(F32)
        grads = (grads * slope_ref[:, span]).astype(BF16)
        grads = nn(first_ref[...], grads).astype(BF16)
        grads = jnp.where(inner_ref[:, span] > 0, grads, jnp.zeros_like(grads))
        grads = nn(two_ref[...], grads).astype(BF16).astype(F32)
        degree = degree_ref[view : view + 1, :]
        wide = grads.shape[0]
        grads = nt(split(grads / degree[:, :seeds]), edges_ref[view, :, :seeds])
        grads = (grads[:wide] + grads[wide:]).astype(BF16)
        grads = jnp.where(hidden_ref[view] > 0, grads, jnp.zeros_like(grads))
        grads = nn(one_ref[...], grads).astype(BF16).astype(F32)
        grads = nt(split(grads / degree), edges_ref[view])
        feature_grads = grads if feature_grads is None else feature_grads + grads
    width = feature_grads.shape[0] // 2
    feature_grads = split(feature_grads[:width] + feature_grads[width:])
    slot_grads = nt(slots_ref[...], feature_grads)
    grads_ref[...] = (slot_grads[:, :width] + slot_grads[:, width:]).astype(BF16)


def slabs_kernel(flat_ref, out_ref):
    slabs, slots = out_ref.shape
    for slab in range(slabs):
        out_ref[slab : slab + 1, :] = flat_ref[:, slab * slots : (slab + 1) * slots]


def fetch_kernel(
    asked_ref, table_far, out_ref, table_ref, wide_ref, rows_ref, index_ref, sem, table_sem
):
    slabs, slots = index_ref.shape
    copy = pltpu.make_async_copy(asked_ref, index_ref, sem)
    copy.start()
    table_copies = slot_parts(table_far, table_ref, table_sem)
    for table_copy in table_copies:
        table_copy.start()
    part = table_ref.shape[0] // len(table_copies)
    for place, table_copy in enumerate(table_copies):
        table_copy.wait()
        span = slice(place * part, (place + 1) * part)
        wide_ref[span, :] = table_ref[span, :].astype(F32)
    copy.wait()

    def step(slab, carry):
        start = pl.multiple_of(slab * slots, slots)
        for slot in range(slots):
            row = jnp.maximum(index_ref[slab, slot], 0)
            rows_ref[pl.ds(start + slot, 1), :] = wide_ref[pl.ds(row, 1), :]
        return carry

    lax.fori_loop(0, slabs, step, 0)
    out_ref[...] = rows_ref[...].astype(BF16).reshape(out_ref.shape)


def scatter_kernel(*refs, spans, first):
    out_ref = refs[-1]
    parts = 4
    rows = out_ref.shape[0] // parts
    picks, pieces = [], []
    for place, span in enumerate(spans):
        row_ref, lane_ref, grads_ref = refs[3 * place : 3 * place + 3]
        low = row_ref[:, span] & (rows - 1)
        hit = low == lax.broadcasted_iota(jnp.int32, (rows, low.shape[1]), 0)
        pick = jnp.where(hit, 1.0, 0.0).astype(BF16)
        grads = grads_ref[...]
        part_of = lane_ref[span, :]
        zero = jnp.zeros_like(grads)
        chosen = [jnp.where(part_of == part, grads, zero) for part in range(parts)]
        picks.append(pick)
        pieces.append(jnp.concatenate(chosen, axis=1))
    added = sum(nn(pick, chosen) for pick, chosen in zip(picks, pieces))
    width = out_ref.shape[1]
    for part in range(parts):
        span = slice(part * rows, (part + 1) * rows)
        value = added[:, part * width : (part + 1) * width]
        out_ref[span, :] = value if first else value + refs[-2][span, :]


def body(
    embedding_table,
    request_rows,
    node_slots,
    neighbours,
    kept_edges,
    weight_one,
    weight_two,
    proj_first,
    proj_second,
):
    table_count = lax.axis_size("table")
    batch_count = lax.axis_size("batch")
    shard_rows, width = embedding_table.shape
    nodes = neighbours.shape[0]
    seeds = SEED_DEV
    slot_count = request_rows.size
    (requests,) = call(
        slabs_kernel,
        [jax.ShapeDtypeStruct((table_count, slot_count // table_count), jnp.int32)],
        [request_rows],
        flops=1000,
        moved=50_000,
        mib=2,
    )

    def turn(value, by):
        return lax.ppermute(
            value, "batch", [(source, (source + by) % batch_count) for source in range(batch_count)]
        )

    received = lax.all_to_all(requests, "table", split_axis=0, concat_axis=0, tiled=True)
    (fetched,) = call(
        fetch_kernel,
        [jax.ShapeDtypeStruct(requests.shape + (width,), BF16)],
        [received, embedding_table],
        flops=1_000_000,
        moved=6_000_000,
        mib=60,
        scratch=[
            pltpu.VMEM((shard_rows, width), BF16),
            pltpu.VMEM((shard_rows, width), F32),
            pltpu.VMEM((slot_count, width), F32),
            pltpu.SMEM(requests.shape, jnp.int32),
            pltpu.SemaphoreType.DMA,
            pltpu.SemaphoreType.DMA((8,)),
        ],
        far=(1,),
    )
    arrived = lax.all_to_all(fetched, "table", split_axis=0, concat_axis=0, tiled=True)

    (slots,) = call(
        slots_kernel,
        [jax.ShapeDtypeStruct((slot_count, nodes), BF16)],
        [node_slots.T],
        flops=10_000_000,
        moved=2 * nodes * slot_count,
        mib=60,
        scratch=[
            pltpu.VMEM((slot_count, nodes), BF16),
            pltpu.SemaphoreType.DMA((nodes // LANES,)),
        ],
        far_outs=(0,),
    )
    kept = kept_edges.transpose(0, 2, 1).astype(F32)
    degree = 1.0 + jnp.sum(kept, axis=1)
    fetched, received, near, kept = lax.optimization_barrier(
        (fetched, received, neighbours.T, kept)
    )
    (edges,) = call(
        edges_kernel,
        [jax.ShapeDtypeStruct((2, nodes, nodes), BF16)],
        [near, kept],
        flops=60_000_000,
        moved=4 * nodes * nodes,
        mib=60,
        scratch=[
            pltpu.VMEM((2, nodes, nodes), BF16),
            pltpu.SemaphoreType.DMA((nodes // LANES,)),
        ],
        far_outs=(0,),
    )
    out_rows = shard_rows // batch_count
    part_rows = out_rows // 4
    offset = lax.axis_index("batch") * out_rows
    owned = []
    for by in range(batch_count):
        index = (received if by == 0 else turn(received, by)).reshape(-1) - offset
        part_of = jnp.where(index < 0, -1, index // part_rows).astype(BF16)
        owned.append((index[None, :], part_of))
    arrived, owned, edges, slots, degree = lax.optimization_barrier(
        (arrived, owned, edges, slots, degree)
    )
    rows = arrived.reshape(slot_count, width)

    wide = weight_one.shape[1]
    keys, raw, hidden, inner, slope = call(
        forward_kernel,
        [
            jax.ShapeDtypeStruct((wide, 2 * seeds), BF16),
            jax.ShapeDtypeStruct((wide, 2 * seeds), F32),
            jax.ShapeDtypeStruct((2, wide, nodes), BF16),
            jax.ShapeDtypeStruct((wide, 2 * seeds), BF16),
            jax.ShapeDtypeStruct((wide, 2 * seeds), F32),
        ],
        [rows, slots, edges, degree, weight_one, weight_two, proj_first, proj_second],
        flops=2_400_000_000,
        moved=10_000_000,
        mib=24,
    )
    ahead, far, behind = [turn(keys, by) for by in (1, 2, 3)]
    keys, owned = lax.optimization_barrier((keys, owned))
    lanes = [jnp.broadcast_to(part_of[:, None], (slot_count, width)) for _, part_of in owned]
    ahead, behind, lanes = lax.optimization_barrier((ahead, behind, lanes))
    owned = [(index, lane) for (index, _), lane in zip(owned, lanes)]
    expo, total0, totals = call(
        early_kernel,
        [
            jax.ShapeDtypeStruct((6 * seeds, 2 * seeds), F32),
            jax.ShapeDtypeStruct((1, 2 * seeds), F32),
            jax.ShapeDtypeStruct((4 * seeds, 1), F32),
        ],
        [keys, ahead, behind],
        flops=800_000_000,
        moved=4_000_000,
        mib=16,
    )
    (grads,) = call(
        backward_kernel,
        [jax.ShapeDtypeStruct((slot_count, width), BF16)],
        [
            keys, ahead, behind, far, expo, total0, totals, raw, hidden, inner, slope,
            slots, edges, degree, weight_one, weight_two, proj_first, proj_second,
        ],
        flops=8_000_000_000,
        moved=12_000_000,
        mib=32,
    )
    returned = lax.all_to_all(
        grads.reshape(table_count, -1, width), "table", split_axis=0, concat_axis=0, tiled=True
    ).reshape(slot_count, width)

    half = slot_count // 2
    upper, lower = slice(0, half), slice(half, slot_count)
    from_left = [turn(returned[upper], 1)]
    from_right = [turn(returned[lower], 3)]
    from_left.append(turn(returned[lower], 1))
    from_right.append(turn(returned[upper], 3))
    from_far = [turn(from_left[0], 1), turn(from_right[0], 3)]
    rounds = (
        ((0, slice(0, slot_count), returned),),
        ((1, upper, from_left[0]), (3, lower, from_right[0])),
        ((1, lower, from_left[1]), (3, upper, from_right[1])),
        ((2, upper, from_far[0]), (2, lower, from_far[1])),
    )
    total = None
    for pieces in rounds:
        args = []
        for source, span, piece in pieces:
            args += [*owned[source], piece]
        args += [] if total is None else [total]
        (total,) = call(
            functools.partial(
                scatter_kernel, spans=[span for _, span, _ in pieces], first=total is None
            ),
            [jax.ShapeDtypeStruct((out_rows, width), F32)],
            args,
            flops=1_000_000_000,
            moved=4_000_000,
            mib=16,
        )
    return total


def solution(mesh):
    in_specs = (
        P("table", None),
        P(("table", "batch"), None),
        P(("table", "batch"), None),
        P(("table", "batch"), None),
        P(None, ("table", "batch"), None),
        P(),
        P(),
        P(),
        P(),
    )
    out_specs = P(("table", "batch"), None)
    return jax.shard_map(body, mesh=mesh, in_specs=in_specs, out_specs=out_specs, check_vma=False)
```

```python
import functools

import jax
import jax.numpy as jnp
from jax import lax
from jax.experimental import pallas as pl
from jax.experimental.pallas import tpu as pltpu
from jax.sharding import PartitionSpec as P

SEED_DEV = 256
TEMPER = 0.25
EPSILON = 1e-06
F32 = jnp.float32
BF16 = jnp.bfloat16
F8 = jnp.float8_e4m3fn
VMEM = pl.BlockSpec(memory_space=pltpu.VMEM)
HBM = pl.BlockSpec(memory_space=pltpu.HBM)


def nn(left, right):
    return lax.dot_general(left, right, (((1,), (0,)), ((), ())), preferred_element_type=F32)


def nt(left, right):
    return lax.dot_general(left, right, (((1,), (1,)), ((), ())), preferred_element_type=F32)


def tn(left, right):
    return lax.dot_general(left, right, (((0,), (0,)), ((), ())), preferred_element_type=F32)


def split(values):
    high = values.astype(BF16)
    low = (values - high.astype(F32)).astype(BF16)
    return jnp.concatenate([high, low], axis=0)


def call(kernel, outs, args, flops, moved, mib, scratch=(), far=(), far_outs=()):
    return pl.pallas_call(
        kernel,
        out_shape=outs,
        in_specs=[
            HBM if place in far else VMEM for place in range(len(args))
        ],
        out_specs=[HBM if place in far_outs else VMEM for place in range(len(outs))],
        scratch_shapes=list(scratch),
        compiler_params=pltpu.CompilerParams(vmem_limit_bytes=mib * 1024 * 1024),
        cost_estimate=pl.CostEstimate(flops=flops, bytes_accessed=moved, transcendentals=0),
    )(*args)


TILE, LANES, ROWS = 32, 128, 64


def spread(row, kind):
    return jnp.broadcast_to(row, (TILE, LANES)).astype(kind)


def places(axis):
    return lax.broadcasted_iota(jnp.int32, (TILE, LANES), axis)


def edges_kernel(near_ref, kept_ref, edges_far, edges_ref, sem):
    views, degree, nodes = kept_ref.shape
    none = jnp.zeros((), BF16)
    copies = []
    for part in range(nodes // LANES):
        span = slice(part * LANES, (part + 1) * LANES)
        nears = [spread(near_ref[slot : slot + 1, span], jnp.int16) for slot in range(degree)]
        kept = [
            [spread(kept_ref[view, slot : slot + 1, span], BF16) for slot in range(degree)]
            for view in range(views)
        ]

        def step(block, carry):
            for tile in range(ROWS // TILE):
                start = pl.multiple_of(block * ROWS + tile * TILE, TILE)
                ids = places(0) + start
                own = jnp.where(ids == places(1) + part * LANES, 1.0, 0.0).astype(BF16)
                ids = ids.astype(jnp.int16)
                totals = [own] * views
                for slot in range(degree):
                    hit = nears[slot] == ids
                    for view in range(views):
                        totals[view] = totals[view] + jnp.where(hit, kept[view][slot], none)
                for view in range(views):
                    edges_ref[view, pl.ds(start, TILE), span] = totals[view].astype(F8)
            return carry

        lax.fori_loop(0, nodes // ROWS, step, 0)
        copies.append(
            pltpu.make_async_copy(edges_ref.at[:, :, span], edges_far.at[:, :, span], sem.at[part])
        )
        copies[-1].start()
    for copy in copies:
        copy.wait()


def slots_kernel(slot_ref, slots_far, slots_ref, sem):
    hashes, nodes = slot_ref.shape
    one, none = jnp.ones((), BF16), jnp.zeros((), BF16)
    copies = []
    for part in range(nodes // LANES):
        span = slice(part * LANES, (part + 1) * LANES)
        named = [spread(slot_ref[which : which + 1, span], jnp.int16) for which in range(hashes)]

        def step(block, carry):
            for tile in range(ROWS // TILE):
                start = pl.multiple_of(block * ROWS + tile * TILE, TILE)
                ids = (places(0) + start).astype(jnp.int16)
                total = jnp.where(named[0] == ids, one, none)
                for which in range(1, hashes):
                    total = total + jnp.where(named[which] == ids, one, none)
                slots_ref[pl.ds(start, TILE), span] = total.astype(F8)
            return carry

        lax.fori_loop(0, slots_ref.shape[0] // ROWS, step, 0)
        copies.append(
            pltpu.make_async_copy(slots_ref.at[:, span], slots_far.at[:, span], sem.at[part])
        )
        copies[-1].start()
    for copy in copies:
        copy.wait()


def slot_parts(source, target, sems):
    count = sems.shape[0]
    part = target.shape[0] // count
    spans = [pl.ds(place * part, part) for place in range(count)]
    return [
        pltpu.make_async_copy(source.at[span], target.at[span], sems.at[place])
        for place, span in enumerate(spans)
    ]


def forward_kernel(
    rows_ref, slots_ref, edges_ref, degree_ref, one_ref, two_ref, first_ref, second_ref,
    keys_ref, raw_ref, hidden_ref, inner_ref, slope_ref, wide_slots_ref, wide_edges_ref,
):
    seeds = SEED_DEV
    width = rows_ref.shape[1]
    slots = slots_ref[...].astype(BF16)
    wide_slots_ref[...] = slots
    features = split(tn(rows_ref[...], slots))
    for view in range(2):
        edges = edges_ref[view].astype(BF16)
        wide_edges_ref[view] = edges
        degree = degree_ref[view : view + 1, :]
        summed = nn(features, edges)
        layer_in = ((summed[:width] + summed[width:]) / degree).astype(BF16)
        hidden = jnp.maximum(tn(one_ref[...], layer_in), 0.0).astype(BF16)
        hidden_ref[view] = hidden
        seed_in = (nn(hidden, edges[:, :seeds]) / degree[:, :seeds]).astype(BF16)
        inner = jnp.maximum(tn(two_ref[...], seed_in), 0.0).astype(BF16)
        before = tn(first_ref[...], inner)
        grown = jnp.exp(jnp.minimum(before, 0.0))
        near_zero = before * (1.0 + before * (0.5 + before * (1.0 / 6.0)))
        below = jnp.where(before > -0.01, near_zero, grown - 1.0)
        projected = jnp.where(before > 0.0, before, below).astype(BF16)
        raw = tn(second_ref[...], projected)
        scale = lax.rsqrt(jnp.sum(raw * raw, axis=0, keepdims=True) + EPSILON)
        span = slice(view * seeds, (view + 1) * seeds)
        keys_ref[:, span] = (raw * scale).astype(BF16)
        raw_ref[:, span] = raw
        inner_ref[:, span] = inner
        slope_ref[:, span] = jnp.where(before > 0.0, 1.0, grown)


def flip(row):
    return jnp.broadcast_to(row, (128, row.shape[1])).T[:, :1]


def pair_expo(left, right_t, same=None):
    expo = jnp.exp(nn(left, right_t) * (1.0 / TEMPER))
    return expo if same is None else jnp.where(same, 0.0, expo)


def diagonal(count):
    down = lax.broadcasted_iota(jnp.int32, (count, count), 0)
    return down == lax.broadcasted_iota(jnp.int32, (count, count), 1)


def down_sum(expo):
    return jnp.sum(expo, axis=0, keepdims=True)


def across_sum(expo):
    return jnp.sum(expo, axis=1, keepdims=True)


def early_kernel(key0_ref, key1_ref, key3_ref, expo_ref, total0_ref, totals_ref):
    own, ahead, behind = key0_ref[...], key1_ref[...], key3_ref[...]
    count = own.shape[1]
    same = diagonal(count)
    expo = pair_expo(own.T, own, same)
    expo_ref[:count, :] = expo
    total0 = down_sum(expo)
    left = ahead.T
    expo = pair_expo(left, own)
    expo_ref[count : 2 * count, :] = expo
    total0 = total0 + down_sum(expo)
    total1 = across_sum(expo) + across_sum(pair_expo(left, ahead, same))
    left = behind.T
    expo = pair_expo(left, own)
    expo_ref[2 * count :, :] = expo
    total0 = total0 + down_sum(expo)
    total3 = across_sum(expo) + across_sum(pair_expo(left, behind, same))
    expo = pair_expo(left, ahead)
    total3 = total3 + across_sum(expo)
    total1 = total1 + flip(down_sum(expo))
    total0_ref[...] = total0
    totals_ref[:count, :] = total1
    totals_ref[count:, :] = total3


def backward_kernel(
    key0_ref, key1_ref, key3_ref, key2_ref, expo_ref, total0_ref, totals_ref,
    raw_ref, hidden_ref, inner_ref, slope_ref,
    slots_ref, edges_ref, degree_ref, one_ref, two_ref, first_ref, second_ref,
    grads_ref,
):
    seeds = SEED_DEV
    far = key2_ref[...]
    count = far.shape[1]
    left = far.T
    last = pair_expo(left, key0_ref[...])
    total0 = total0_ref[...] + down_sum(last)
    total2 = across_sum(last) + across_sum(pair_expo(left, far, diagonal(count)))
    expo = pair_expo(left, key1_ref[...])
    total2 = total2 + across_sum(expo)
    total1 = totals_ref[:count, :] + flip(down_sum(expo))
    expo = pair_expo(left, key3_ref[...])
    total2 = total2 + across_sum(expo)
    total3 = totals_ref[count:, :] + flip(down_sum(expo))
    own_inverse = 1.0 / total0
    pulled = jnp.zeros(far.shape, F32)
    blocks = (
        (key0_ref, expo_ref[:count, :], flip(total0)),
        (key1_ref, expo_ref[count : 2 * count, :], total1),
        (key3_ref, expo_ref[2 * count :, :], total3),
        (key2_ref, last, total2),
    )
    for key_ref, expo, total in blocks:
        weights = (expo * (own_inverse + 1.0 / total)).astype(BF16)
        pulled = pulled + nn(key_ref[...], weights)
    feature_grads = None
    for view in range(2):
        span = slice(view * seeds, (view + 1) * seeds)
        other = slice((1 - view) * seeds, (2 - view) * seeds)
        partner = key0_ref[:, other].astype(F32)
        key_grads = (pulled[:, span] - 2.0 * partner) * (1.0 / TEMPER)
        raw = raw_ref[:, span]
        scale = lax.rsqrt(jnp.sum(raw * raw, axis=0, keepdims=True) + EPSILON)
        along = jnp.sum(raw * key_grads, axis=0, keepdims=True) * (scale * scale)
        raw_grads = ((key_grads - raw * along) * scale).astype(BF16)
        grads = nn(second_ref[...], raw_grads).astype(BF16).astype(F32)
        grads = (grads * slope_ref[:, span]).astype(BF16)
        grads = nn(first_ref[...], grads).astype(BF16)
        grads = jnp.where(inner_ref[:, span] > 0, grads, jnp.zeros_like(grads))
        grads = nn(two_ref[...], grads).astype(BF16).astype(F32)
        degree = degree_ref[view : view + 1, :]
        wide = grads.shape[0]
        grads = nt(split(grads / degree[:, :seeds]), edges_ref[view, :, :seeds])
        grads = (grads[:wide] + grads[wide:]).astype(BF16)
        grads = jnp.where(hidden_ref[view] > 0, grads, jnp.zeros_like(grads))
        grads = nn(one_ref[...], grads).astype(BF16).astype(F32)
        grads = nt(split(grads / degree), edges_ref[view])
        feature_grads = grads if feature_grads is None else feature_grads + grads
    width = feature_grads.shape[0] // 2
    feature_grads = split(feature_grads[:width] + feature_grads[width:])
    slot_grads = nt(slots_ref[...], feature_grads)
    grads_ref[...] = (slot_grads[:, :width] + slot_grads[:, width:]).astype(BF16)


def slabs_kernel(flat_ref, out_ref):
    slabs, slots = out_ref.shape
    for slab in range(slabs):
        out_ref[slab : slab + 1, :] = flat_ref[:, slab * slots : (slab + 1) * slots]


def fetch_kernel(
    asked_far, table_far, out_ref, table_ref, wide_ref, rows_ref, index_ref, sem, table_sem
):
    slabs, slots = index_ref.shape
    copy = pltpu.make_async_copy(asked_far, index_ref, sem)
    copy.start()
    table_copies = slot_parts(table_far, table_ref, table_sem)
    for table_copy in table_copies:
        table_copy.start()
    part = table_ref.shape[0] // len(table_copies)
    for place, table_copy in enumerate(table_copies):
        table_copy.wait()
        span = slice(place * part, (place + 1) * part)
        wide_ref[span, :] = table_ref[span, :].astype(F32)
    copy.wait()

    def step(slab, carry):
        start = pl.multiple_of(slab * slots, slots)
        for slot in range(slots):
            row = jnp.maximum(index_ref[slab, slot], 0)
            rows_ref[pl.ds(start + slot, 1), :] = wide_ref[pl.ds(row, 1), :]
        return carry

    lax.fori_loop(0, slabs, step, 0)
    out_ref[...] = rows_ref[...].astype(BF16).reshape(out_ref.shape)


def scatter_kernel(*refs, spans, first):
    out_ref = refs[-1]
    parts = 4
    rows = out_ref.shape[0] // parts
    picks, pieces = [], []
    for place, span in enumerate(spans):
        row_ref, lane_ref, grads_ref = refs[3 * place : 3 * place + 3]
        low = row_ref[:, span] & (rows - 1)
        hit = low == lax.broadcasted_iota(jnp.int32, (rows, low.shape[1]), 0)
        pick = jnp.where(hit, 1.0, 0.0).astype(BF16)
        grads = grads_ref[...]
        part_of = lane_ref[span, :]
        zero = jnp.zeros_like(grads)
        chosen = [jnp.where(part_of == part, grads, zero) for part in range(parts)]
        picks.append(pick)
        pieces.append(jnp.concatenate(chosen, axis=1))
    added = sum(nn(pick, chosen) for pick, chosen in zip(picks, pieces))
    width = out_ref.shape[1]
    for part in range(parts):
        span = slice(part * rows, (part + 1) * rows)
        value = added[:, part * width : (part + 1) * width]
        out_ref[span, :] = value if first else value + refs[-2][span, :]


def body(
    embedding_table,
    request_rows,
    node_slots,
    neighbours,
    kept_edges,
    weight_one,
    weight_two,
    proj_first,
    proj_second,
):
    table_count = lax.axis_size("table")
    batch_count = lax.axis_size("batch")
    shard_rows, width = embedding_table.shape
    nodes = neighbours.shape[0]
    seeds = SEED_DEV
    slot_count = request_rows.size
    (requests,) = call(
        slabs_kernel,
        [jax.ShapeDtypeStruct((table_count, slot_count // table_count), jnp.int32)],
        [request_rows],
        flops=1000,
        moved=50_000,
        mib=2,
    )

    def turn(value, by):
        return lax.ppermute(
            value, "batch", [(source, (source + by) % batch_count) for source in range(batch_count)]
        )

    received = lax.all_to_all(requests, "table", split_axis=0, concat_axis=0, tiled=True)
    (fetched,) = call(
        fetch_kernel,
        [jax.ShapeDtypeStruct(requests.shape + (width,), BF16)],
        [received, embedding_table],
        flops=1_000_000,
        moved=6_000_000,
        mib=60,
        scratch=[
            pltpu.VMEM((shard_rows, width), BF16),
            pltpu.VMEM((shard_rows, width), F32),
            pltpu.VMEM((slot_count, width), F32),
            pltpu.SMEM(requests.shape, jnp.int32),
            pltpu.SemaphoreType.DMA,
            pltpu.SemaphoreType.DMA((8,)),
        ],
        far=(0, 1),
    )
    arrived = lax.all_to_all(fetched, "table", split_axis=0, concat_axis=0, tiled=True)

    (slots,) = call(
        slots_kernel,
        [jax.ShapeDtypeStruct((slot_count, nodes), F8)],
        [node_slots.T],
        flops=10_000_000,
        moved=2 * nodes * slot_count,
        mib=60,
        scratch=[
            pltpu.VMEM((slot_count, nodes), F8),
            pltpu.SemaphoreType.DMA((nodes // LANES,)),
        ],
        far_outs=(0,),
    )
    fetched, received, near, kept = lax.optimization_barrier(
        (fetched, received, neighbours.T, kept_edges)
    )
    kept = kept.transpose(0, 2, 1).astype(F32)
    degree = 1.0 + jnp.sum(kept, axis=1)
    (edges,) = call(
        edges_kernel,
        [jax.ShapeDtypeStruct((2, nodes, nodes), F8)],
        [near, kept],
        flops=60_000_000,
        moved=4 * nodes * nodes,
        mib=60,
        scratch=[
            pltpu.VMEM((2, nodes, nodes), F8),
            pltpu.SemaphoreType.DMA((nodes // LANES,)),
        ],
        far_outs=(0,),
    )
    out_rows = shard_rows // batch_count
    part_rows = out_rows // 4
    offset = lax.axis_index("batch") * out_rows
    owned = []
    for by in range(batch_count):
        index = (received if by == 0 else turn(received, by)).reshape(-1) - offset
        part_of = jnp.where(index < 0, -1, index // part_rows).astype(BF16)
        owned.append((index[None, :], part_of))
    arrived, owned, edges, slots, degree = lax.optimization_barrier(
        (arrived, owned, edges, slots, degree)
    )
    rows = arrived.reshape(slot_count, width)

    wide = weight_one.shape[1]
    keys, raw, hidden, inner, slope, slots, edges = call(
        forward_kernel,
        [
            jax.ShapeDtypeStruct((wide, 2 * seeds), BF16),
            jax.ShapeDtypeStruct((wide, 2 * seeds), F32),
            jax.ShapeDtypeStruct((2, wide, nodes), BF16),
            jax.ShapeDtypeStruct((wide, 2 * seeds), BF16),
            jax.ShapeDtypeStruct((wide, 2 * seeds), F32),
            jax.ShapeDtypeStruct((slot_count, nodes), BF16),
            jax.ShapeDtypeStruct((2, nodes, nodes), BF16),
        ],
        [rows, slots, edges, degree, weight_one, weight_two, proj_first, proj_second],
        flops=2_400_000_000,
        moved=10_000_000,
        mib=32,
    )
    ahead, far, behind = [turn(keys, by) for by in (1, 2, 3)]
    keys, owned = lax.optimization_barrier((keys, owned))
    lanes = [jnp.broadcast_to(part_of[:, None], (slot_count, width)) for _, part_of in owned]
    ahead, behind, lanes = lax.optimization_barrier((ahead, behind, lanes))
    owned = [(index, lane) for (index, _), lane in zip(owned, lanes)]
    expo, total0, totals = call(
        early_kernel,
        [
            jax.ShapeDtypeStruct((6 * seeds, 2 * seeds), F32),
            jax.ShapeDtypeStruct((1, 2 * seeds), F32),
            jax.ShapeDtypeStruct((4 * seeds, 1), F32),
        ],
        [keys, ahead, behind],
        flops=800_000_000,
        moved=4_000_000,
        mib=16,
    )
    (grads,) = call(
        backward_kernel,
        [jax.ShapeDtypeStruct((slot_count, width), BF16)],
        [
            keys, ahead, behind, far, expo, total0, totals, raw, hidden, inner, slope,
            slots, edges, degree, weight_one, weight_two, proj_first, proj_second,
        ],
        flops=8_000_000_000,
        moved=12_000_000,
        mib=32,
    )
    returned = lax.all_to_all(
        grads.reshape(table_count, -1, width), "table", split_axis=0, concat_axis=0, tiled=True
    ).reshape(slot_count, width)

    half = slot_count // 2
    upper, lower = slice(0, half), slice(half, slot_count)
    from_left = [turn(returned[upper], 1)]
    from_right = [turn(returned[lower], 3)]
    from_left.append(turn(returned[lower], 1))
    from_right.append(turn(returned[upper], 3))
    from_far = [turn(from_left[0], 1), turn(from_right[0], 3)]
    rounds = (
        ((0, slice(0, slot_count), returned),),
        ((1, upper, from_left[0]), (3, lower, from_right[0])),
        ((1, lower, from_left[1]), (3, upper, from_right[1])),
        ((2, upper, from_far[0]), (2, lower, from_far[1])),
    )
    total = None
    for pieces in rounds:
        args = []
        for source, span, piece in pieces:
            args += [*owned[source], piece]
        args += [] if total is None else [total]
        (total,) = call(
            functools.partial(
                scatter_kernel, spans=[span for _, span, _ in pieces], first=total is None
            ),
            [jax.ShapeDtypeStruct((out_rows, width), F32)],
            args,
            flops=1_000_000_000,
            moved=4_000_000,
            mib=16,
        )
    return total


def solution(mesh):
    in_specs = (
        P("table", None),
        P(("table", "batch"), None),
        P(("table", "batch"), None),
        P(("table", "batch"), None),
        P(None, ("table", "batch"), None),
        P(),
        P(),
        P(),
        P(),
    )
    out_specs = P(("table", "batch"), None)
    return jax.shard_map(body, mesh=mesh, in_specs=in_specs, out_specs=out_specs, check_vma=False)
```

```python
import functools

import jax
import jax.numpy as jnp
from jax import lax
from jax.experimental import pallas as pl
from jax.experimental.pallas import tpu as pltpu
from jax.sharding import PartitionSpec as P

SEED_DEV = 256
TEMPER = 0.25
EPSILON = 1e-06
F32 = jnp.float32
BF16 = jnp.bfloat16
F8 = jnp.float8_e4m3fn
VMEM = pl.BlockSpec(memory_space=pltpu.VMEM)
HBM = pl.BlockSpec(memory_space=pltpu.HBM)


def nn(left, right):
    return lax.dot_general(left, right, (((1,), (0,)), ((), ())), preferred_element_type=F32)


def nt(left, right):
    return lax.dot_general(left, right, (((1,), (1,)), ((), ())), preferred_element_type=F32)


def tn(left, right):
    return lax.dot_general(left, right, (((0,), (0,)), ((), ())), preferred_element_type=F32)


def split(values):
    high = values.astype(BF16)
    low = (values - high.astype(F32)).astype(BF16)
    return jnp.concatenate([high, low], axis=0)


def call(kernel, outs, args, flops, moved, mib, scratch=(), far=(), far_outs=()):
    return pl.pallas_call(
        kernel,
        out_shape=outs,
        in_specs=[
            HBM if place in far else VMEM for place in range(len(args))
        ],
        out_specs=[HBM if place in far_outs else VMEM for place in range(len(outs))],
        scratch_shapes=list(scratch),
        compiler_params=pltpu.CompilerParams(vmem_limit_bytes=mib * 1024 * 1024),
        cost_estimate=pl.CostEstimate(flops=flops, bytes_accessed=moved, transcendentals=0),
    )(*args)


TILE, LANES, ROWS = 32, 128, 128


def spread(row, kind):
    return jnp.broadcast_to(row, (TILE, LANES)).astype(kind)


def places(axis):
    return lax.broadcasted_iota(jnp.int32, (TILE, LANES), axis)


def edges_kernel(near_ref, kept_ref, edges_far, edges_ref, sem):
    views, degree, nodes = kept_ref.shape
    none = jnp.zeros((), BF16)
    copies = []
    for part in range(nodes // LANES):
        span = slice(part * LANES, (part + 1) * LANES)
        nears = [spread(near_ref[slot : slot + 1, span], jnp.int16) for slot in range(degree)]
        kept = [
            [spread(kept_ref[view, slot : slot + 1, span], BF16) for slot in range(degree)]
            for view in range(views)
        ]

        def step(block, carry):
            for tile in range(ROWS // TILE):
                start = pl.multiple_of(block * ROWS + tile * TILE, TILE)
                ids = places(0) + start
                own = jnp.where(ids == places(1) + part * LANES, 1.0, 0.0).astype(BF16)
                ids = ids.astype(jnp.int16)
                totals = [own] * views
                for slot in range(degree):
                    hit = nears[slot] == ids
                    for view in range(views):
                        totals[view] = totals[view] + jnp.where(hit, kept[view][slot], none)
                for view in range(views):
                    edges_ref[view, pl.ds(start, TILE), span] = totals[view].astype(F8)
            return carry

        lax.fori_loop(0, nodes // ROWS, step, 0)
        copies.append(
            pltpu.make_async_copy(edges_ref.at[:, :, span], edges_far.at[:, :, span], sem.at[part])
        )
        copies[-1].start()
    for copy in copies:
        copy.wait()


def slots_kernel(slot_ref, slots_far, slots_ref, sem):
    hashes, nodes = slot_ref.shape
    rows = min(256, slots_ref.shape[0])
    one, none = jnp.ones((), BF16), jnp.zeros((), BF16)
    copies = []
    for part in range(nodes // LANES):
        span = slice(part * LANES, (part + 1) * LANES)
        named = [spread(slot_ref[which : which + 1, span], jnp.int16) for which in range(hashes)]

        def step(block, carry):
            for tile in range(rows // TILE):
                start = pl.multiple_of(block * rows + tile * TILE, TILE)
                ids = (places(0) + start).astype(jnp.int16)
                total = jnp.where(named[0] == ids, one, none)
                for which in range(1, hashes):
                    total = total + jnp.where(named[which] == ids, one, none)
                slots_ref[pl.ds(start, TILE), span] = total.astype(F8)
            return carry

        lax.fori_loop(0, slots_ref.shape[0] // rows, step, 0)
        copies.append(
            pltpu.make_async_copy(slots_ref.at[:, span], slots_far.at[:, span], sem.at[part])
        )
        copies[-1].start()
    for copy in copies:
        copy.wait()


def forward_kernel(
    rows_ref, slots_ref, edges_ref, degree_ref, one_ref, two_ref, first_ref, second_ref,
    keys_ref, raw_ref, hidden_ref, inner_ref, slope_ref, wide_slots_ref, wide_edges_ref,
):
    seeds = SEED_DEV
    width = rows_ref.shape[1]
    slots = slots_ref[...].astype(BF16)
    wide_slots_ref[...] = slots
    features = split(tn(rows_ref[...], slots))
    for view in range(2):
        edges = edges_ref[view].astype(BF16)
        wide_edges_ref[view] = edges
        degree = degree_ref[view : view + 1, :]
        summed = nn(features, edges)
        layer_in = ((summed[:width] + summed[width:]) / degree).astype(BF16)
        hidden = jnp.maximum(tn(one_ref[...], layer_in), 0.0).astype(BF16)
        hidden_ref[view] = hidden
        seed_in = (nn(hidden, edges[:, :seeds]) / degree[:, :seeds]).astype(BF16)
        inner = jnp.maximum(tn(two_ref[...], seed_in), 0.0).astype(BF16)
        before = tn(first_ref[...], inner)
        grown = jnp.exp(jnp.minimum(before, 0.0))
        near_zero = before * (1.0 + before * (0.5 + before * (1.0 / 6.0)))
        below = jnp.where(before > -0.01, near_zero, grown - 1.0)
        projected = jnp.where(before > 0.0, before, below).astype(BF16)
        raw = tn(second_ref[...], projected)
        scale = lax.rsqrt(jnp.sum(raw * raw, axis=0, keepdims=True) + EPSILON)
        span = slice(view * seeds, (view + 1) * seeds)
        keys_ref[:, span] = (raw * scale).astype(BF16)
        raw_ref[:, span] = raw
        inner_ref[:, span] = inner
        slope_ref[:, span] = jnp.where(before > 0.0, 1.0, grown)


def flip(row):
    return jnp.broadcast_to(row, (128, row.shape[1])).T[:, :1]


def pair_expo(left, right_t, same=None):
    expo = jnp.exp(nn(left, right_t) * (1.0 / TEMPER))
    return expo if same is None else jnp.where(same, 0.0, expo)


def diagonal(count):
    down = lax.broadcasted_iota(jnp.int32, (count, count), 0)
    return down == lax.broadcasted_iota(jnp.int32, (count, count), 1)


def down_sum(expo):
    return jnp.sum(expo, axis=0, keepdims=True)


def across_sum(expo):
    return jnp.sum(expo, axis=1, keepdims=True)


def early_kernel(key0_ref, key1_ref, key3_ref, expo_ref, total0_ref, totals_ref):
    own, ahead, behind = key0_ref[...], key1_ref[...], key3_ref[...]
    count = own.shape[1]
    same = diagonal(count)
    expo = pair_expo(own.T, own, same)
    expo_ref[:count, :] = expo
    total0 = down_sum(expo)
    left = ahead.T
    expo = pair_expo(left, own)
    expo_ref[count : 2 * count, :] = expo
    total0 = total0 + down_sum(expo)
    total1 = across_sum(expo) + across_sum(pair_expo(left, ahead, same))
    left = behind.T
    expo = pair_expo(left, own)
    expo_ref[2 * count :, :] = expo
    total0 = total0 + down_sum(expo)
    total3 = across_sum(expo) + across_sum(pair_expo(left, behind, same))
    expo = pair_expo(left, ahead)
    total3 = total3 + across_sum(expo)
    total1 = total1 + flip(down_sum(expo))
    total0_ref[...] = total0
    totals_ref[:count, :] = total1
    totals_ref[count:, :] = total3


def backward_kernel(
    key0_ref, key1_ref, key3_ref, key2_ref, expo_ref, total0_ref, totals_ref,
    raw_ref, hidden_ref, inner_ref, slope_ref,
    slots_ref, edges_ref, degree_ref, one_ref, two_ref, first_ref, second_ref,
    grads_ref,
):
    seeds = SEED_DEV
    far = key2_ref[...]
    count = far.shape[1]
    left = far.T
    last = pair_expo(left, key0_ref[...])
    total0 = total0_ref[...] + down_sum(last)
    total2 = across_sum(last) + across_sum(pair_expo(left, far, diagonal(count)))
    expo = pair_expo(left, key1_ref[...])
    total2 = total2 + across_sum(expo)
    total1 = totals_ref[:count, :] + flip(down_sum(expo))
    expo = pair_expo(left, key3_ref[...])
    total2 = total2 + across_sum(expo)
    total3 = totals_ref[count:, :] + flip(down_sum(expo))
    own_inverse = 1.0 / total0
    pulled = jnp.zeros(far.shape, F32)
    blocks = (
        (key0_ref, expo_ref[:count, :], flip(total0)),
        (key1_ref, expo_ref[count : 2 * count, :], total1),
        (key3_ref, expo_ref[2 * count :, :], total3),
        (key2_ref, last, total2),
    )
    for key_ref, expo, total in blocks:
        weights = (expo * (own_inverse + 1.0 / total)).astype(BF16)
        pulled = pulled + nn(key_ref[...], weights)
    feature_grads = None
    for view in range(2):
        span = slice(view * seeds, (view + 1) * seeds)
        other = slice((1 - view) * seeds, (2 - view) * seeds)
        partner = key0_ref[:, other].astype(F32)
        key_grads = (pulled[:, span] - 2.0 * partner) * (1.0 / TEMPER)
        raw = raw_ref[:, span]
        scale = lax.rsqrt(jnp.sum(raw * raw, axis=0, keepdims=True) + EPSILON)
        along = jnp.sum(raw * key_grads, axis=0, keepdims=True) * (scale * scale)
        raw_grads = ((key_grads - raw * along) * scale).astype(BF16)
        grads = nn(second_ref[...], raw_grads).astype(BF16).astype(F32)
        grads = (grads * slope_ref[:, span]).astype(BF16)
        grads = nn(first_ref[...], grads).astype(BF16)
        grads = jnp.where(inner_ref[:, span] > 0, grads, jnp.zeros_like(grads))
        grads = nn(two_ref[...], grads).astype(BF16).astype(F32)
        degree = degree_ref[view : view + 1, :]
        wide = grads.shape[0]
        grads = nt(split(grads / degree[:, :seeds]), edges_ref[view, :, :seeds])
        grads = (grads[:wide] + grads[wide:]).astype(BF16)
        grads = jnp.where(hidden_ref[view] > 0, grads, jnp.zeros_like(grads))
        grads = nn(one_ref[...], grads).astype(BF16).astype(F32)
        grads = nt(split(grads / degree), edges_ref[view])
        feature_grads = grads if feature_grads is None else feature_grads + grads
    width = feature_grads.shape[0] // 2
    feature_grads = split(feature_grads[:width] + feature_grads[width:])
    slot_grads = nt(slots_ref[...], feature_grads)
    grads_ref[...] = (slot_grads[:, :width] + slot_grads[:, width:]).astype(BF16)


def slabs_kernel(flat_ref, out_ref):
    slabs, slots = out_ref.shape
    for slab in range(slabs):
        out_ref[slab : slab + 1, :] = flat_ref[:, slab * slots : (slab + 1) * slots]


def fetch_kernel(
    asked_ref, table_ref, out_ref, again_ref, wide_ref, rows_ref, row_ref, index_ref, sem
):
    slabs, slots = index_ref.shape
    asked = asked_ref[...]
    row_ref[...] = jnp.maximum(asked, 0)
    copy = pltpu.make_async_copy(row_ref, index_ref, sem)
    copy.start()
    again_ref[...] = asked
    wide_ref[...] = table_ref[...].astype(F32)
    copy.wait()

    def step(pair, carry):
        for which in range(2):
            slab = 2 * pair + which
            start = pl.multiple_of(slab * slots, slots)
            for slot in range(slots):
                row = index_ref[slab, slot]
                rows_ref[pl.ds(start + slot, 1), :] = wide_ref[pl.ds(row, 1), :]
        return carry

    lax.fori_loop(0, slabs // 2, step, 0)
    out_ref[...] = rows_ref[...].astype(BF16).reshape(out_ref.shape)


def scatter_kernel(*refs, spans, first):
    out_ref = refs[-1]
    parts = 4
    rows = out_ref.shape[0] // parts
    picks, pieces = [], []
    for place, span in enumerate(spans):
        row_ref, lane_ref, grads_ref = refs[3 * place : 3 * place + 3]
        low = row_ref[:, span] & (rows - 1)
        hit = low == lax.broadcasted_iota(jnp.int32, (rows, low.shape[1]), 0)
        pick = jnp.where(hit, 1.0, 0.0).astype(BF16)
        grads = grads_ref[...]
        part_of = lane_ref[span, :]
        zero = jnp.zeros_like(grads)
        chosen = [jnp.where(part_of == part, grads, zero) for part in range(parts)]
        picks.append(pick)
        pieces.append(jnp.concatenate(chosen, axis=1))
    added = sum(nn(pick, chosen) for pick, chosen in zip(picks, pieces))
    width = out_ref.shape[1]
    for part in range(parts):
        span = slice(part * rows, (part + 1) * rows)
        value = added[:, part * width : (part + 1) * width]
        out_ref[span, :] = value if first else value + refs[-2][span, :]


def body(
    embedding_table,
    request_rows,
    node_slots,
    neighbours,
    kept_edges,
    weight_one,
    weight_two,
    proj_first,
    proj_second,
):
    table_count = lax.axis_size("table")
    batch_count = lax.axis_size("batch")
    shard_rows, width = embedding_table.shape
    nodes = neighbours.shape[0]
    seeds = SEED_DEV
    slot_count = request_rows.size
    (requests,) = call(
        slabs_kernel,
        [jax.ShapeDtypeStruct((table_count, slot_count // table_count), jnp.int32)],
        [request_rows],
        flops=1000,
        moved=50_000,
        mib=2,
    )

    def turn(value, by):
        return lax.ppermute(
            value, "batch", [(source, (source + by) % batch_count) for source in range(batch_count)]
        )

    received = lax.all_to_all(requests, "table", split_axis=0, concat_axis=0, tiled=True)
    (slots,) = call(
        slots_kernel,
        [jax.ShapeDtypeStruct((slot_count, nodes), F8)],
        [node_slots.T],
        flops=10_000_000,
        moved=2 * nodes * slot_count,
        mib=60,
        scratch=[
            pltpu.VMEM((slot_count, nodes), F8),
            pltpu.SemaphoreType.DMA((nodes // LANES,)),
        ],
        far_outs=(0,),
    )
    fetched, received = call(
        fetch_kernel,
        [
            jax.ShapeDtypeStruct(requests.shape + (width,), BF16),
            jax.ShapeDtypeStruct(requests.shape, jnp.int32),
        ],
        [received, embedding_table],
        flops=1_000_000,
        moved=6_000_000,
        mib=24,
        scratch=[
            pltpu.VMEM((shard_rows, width), F32),
            pltpu.VMEM((slot_count, width), F32),
            pltpu.VMEM(requests.shape, jnp.int32),
            pltpu.SMEM(requests.shape, jnp.int32),
            pltpu.SemaphoreType.DMA,
        ],
    )
    arrived = lax.all_to_all(fetched, "table", split_axis=0, concat_axis=0, tiled=True)

    fetched, received, near, kept = lax.optimization_barrier(
        (fetched, received, neighbours.T, kept_edges)
    )
    kept = kept.transpose(0, 2, 1).astype(F32)
    degree = 1.0 + jnp.sum(kept, axis=1)
    (edges,) = call(
        edges_kernel,
        [jax.ShapeDtypeStruct((2, nodes, nodes), F8)],
        [near, kept],
        flops=60_000_000,
        moved=4 * nodes * nodes,
        mib=60,
        scratch=[
            pltpu.VMEM((2, nodes, nodes), F8),
            pltpu.SemaphoreType.DMA((nodes // LANES,)),
        ],
        far_outs=(0,),
    )
    out_rows = shard_rows // batch_count
    part_rows = out_rows // 4
    offset = lax.axis_index("batch") * out_rows
    owned = []
    for by in range(batch_count):
        index = (received if by == 0 else turn(received, by)).reshape(-1) - offset
        part_of = jnp.where(index < 0, -1, index // part_rows).astype(BF16)
        owned.append((index[None, :], part_of))
    arrived, owned, edges, slots, degree = lax.optimization_barrier(
        (arrived, owned, edges, slots, degree)
    )
    rows = arrived.reshape(slot_count, width)

    wide = weight_one.shape[1]
    keys, raw, hidden, inner, slope, slots, edges = call(
        forward_kernel,
        [
            jax.ShapeDtypeStruct((wide, 2 * seeds), BF16),
            jax.ShapeDtypeStruct((wide, 2 * seeds), F32),
            jax.ShapeDtypeStruct((2, wide, nodes), BF16),
            jax.ShapeDtypeStruct((wide, 2 * seeds), BF16),
            jax.ShapeDtypeStruct((wide, 2 * seeds), F32),
            jax.ShapeDtypeStruct((slot_count, nodes), BF16),
            jax.ShapeDtypeStruct((2, nodes, nodes), BF16),
        ],
        [rows, slots, edges, degree, weight_one, weight_two, proj_first, proj_second],
        flops=2_400_000_000,
        moved=10_000_000,
        mib=32,
    )
    ahead, far, behind = [turn(keys, by) for by in (1, 2, 3)]
    expo, total0, totals = call(
        early_kernel,
        [
            jax.ShapeDtypeStruct((6 * seeds, 2 * seeds), F32),
            jax.ShapeDtypeStruct((1, 2 * seeds), F32),
            jax.ShapeDtypeStruct((4 * seeds, 1), F32),
        ],
        [keys, ahead, behind],
        flops=800_000_000,
        moved=4_000_000,
        mib=16,
    )
    (grads,) = call(
        backward_kernel,
        [jax.ShapeDtypeStruct((slot_count, width), BF16)],
        [
            keys, ahead, behind, far, expo, total0, totals, raw, hidden, inner, slope,
            slots, edges, degree, weight_one, weight_two, proj_first, proj_second,
        ],
        flops=8_000_000_000,
        moved=12_000_000,
        mib=32,
    )
    returned = lax.all_to_all(
        grads.reshape(table_count, -1, width), "table", split_axis=0, concat_axis=0, tiled=True
    ).reshape(slot_count, width)

    half = slot_count // 2
    upper, lower = slice(0, half), slice(half, slot_count)
    from_left = [turn(returned[upper], 1)]
    from_right = [turn(returned[lower], 3)]
    from_left[0], owned = lax.optimization_barrier((from_left[0], owned))
    owned = [
        (index, jnp.broadcast_to(part_of[:, None], (slot_count, width))) for index, part_of in owned
    ]
    from_left.append(turn(returned[lower], 1))
    owned[0], owned[2] = lax.optimization_barrier((owned[0], owned[2]))
    from_right.append(turn(returned[upper], 3))
    from_far = [turn(from_left[0], 1), turn(from_right[0], 3)]
    rounds = (
        ((0, slice(0, slot_count), returned),),
        ((1, upper, from_left[0]), (3, lower, from_right[0])),
        ((1, lower, from_left[1]), (3, upper, from_right[1])),
        ((2, upper, from_far[0]), (2, lower, from_far[1])),
    )
    total = None
    for pieces in rounds:
        args = []
        for source, span, piece in pieces:
            args += [*owned[source], piece]
        args += [] if total is None else [total]
        (total,) = call(
            functools.partial(
                scatter_kernel, spans=[span for _, span, _ in pieces], first=total is None
            ),
            [jax.ShapeDtypeStruct((out_rows, width), F32)],
            args,
            flops=1_000_000_000,
            moved=4_000_000,
            mib=16,
        )
    return total


def solution(mesh):
    in_specs = (
        P("table", None),
        P(("table", "batch"), None),
        P(("table", "batch"), None),
        P(("table", "batch"), None),
        P(None, ("table", "batch"), None),
        P(),
        P(),
        P(),
        P(),
    )
    out_specs = P(("table", "batch"), None)
    return jax.shard_map(body, mesh=mesh, in_specs=in_specs, out_specs=out_specs, check_vma=False)
```

```python
import functools

import jax
import jax.numpy as jnp
from jax import lax
from jax.experimental import pallas as pl
from jax.experimental.pallas import tpu as pltpu
from jax.sharding import PartitionSpec as P

SEED_DEV = 256
TEMPER = 0.25
EPSILON = 1e-06
F32 = jnp.float32
BF16 = jnp.bfloat16
F8 = jnp.float8_e4m3fn
VMEM = pl.BlockSpec(memory_space=pltpu.VMEM)
HBM = pl.BlockSpec(memory_space=pltpu.HBM)


def nn(left, right):
    return lax.dot_general(left, right, (((1,), (0,)), ((), ())), preferred_element_type=F32)


def nt(left, right):
    return lax.dot_general(left, right, (((1,), (1,)), ((), ())), preferred_element_type=F32)


def tn(left, right):
    return lax.dot_general(left, right, (((0,), (0,)), ((), ())), preferred_element_type=F32)


def split(values):
    high = values.astype(BF16)
    low = (values - high.astype(F32)).astype(BF16)
    return jnp.concatenate([high, low], axis=0)


def call(kernel, outs, args, flops, moved, mib, scratch=(), far=(), far_outs=()):
    return pl.pallas_call(
        kernel,
        out_shape=outs,
        in_specs=[
            HBM if place in far else VMEM for place in range(len(args))
        ],
        out_specs=[HBM if place in far_outs else VMEM for place in range(len(outs))],
        scratch_shapes=list(scratch),
        compiler_params=pltpu.CompilerParams(vmem_limit_bytes=mib * 1024 * 1024),
        cost_estimate=pl.CostEstimate(flops=flops, bytes_accessed=moved, transcendentals=0),
    )(*args)


TILE, LANES, ROWS = 32, 128, 128


def spread(row, kind):
    return jnp.broadcast_to(row, (TILE, LANES)).astype(kind)


def places(axis):
    return lax.broadcasted_iota(jnp.int32, (TILE, LANES), axis)


def edges_kernel(near_ref, kept_ref, edges_far, edges_ref, sem):
    views, degree, nodes = kept_ref.shape
    none = jnp.zeros((), BF16)
    copies = []
    for part in range(nodes // LANES):
        span = slice(part * LANES, (part + 1) * LANES)
        nears = [spread(near_ref[slot : slot + 1, span], jnp.int16) for slot in range(degree)]
        kept = [
            [spread(kept_ref[view, slot : slot + 1, span], BF16) for slot in range(degree)]
            for view in range(views)
        ]

        def step(block, carry):
            for tile in range(ROWS // TILE):
                start = pl.multiple_of(block * ROWS + tile * TILE, TILE)
                ids = places(0) + start
                own = jnp.where(ids == places(1) + part * LANES, 1.0, 0.0).astype(BF16)
                ids = ids.astype(jnp.int16)
                totals = [own] * views
                for slot in range(degree):
                    hit = nears[slot] == ids
                    for view in range(views):
                        totals[view] = totals[view] + jnp.where(hit, kept[view][slot], none)
                for view in range(views):
                    edges_ref[view, pl.ds(start, TILE), span] = totals[view].astype(F8)
            return carry

        lax.fori_loop(0, nodes // ROWS, step, 0)
        copies.append(
            pltpu.make_async_copy(edges_ref.at[:, :, span], edges_far.at[:, :, span], sem.at[part])
        )
        copies[-1].start()
    for copy in copies:
        copy.wait()


def slots_kernel(slot_ref, slots_far, slots_ref, sem):
    hashes, nodes = slot_ref.shape
    rows = min(256, slots_ref.shape[0])
    one, none = jnp.ones((), BF16), jnp.zeros((), BF16)
    copies = []
    for part in range(nodes // LANES):
        span = slice(part * LANES, (part + 1) * LANES)
        named = [spread(slot_ref[which : which + 1, span], jnp.int16) for which in range(hashes)]

        def step(block, carry):
            for tile in range(rows // TILE):
                start = pl.multiple_of(block * rows + tile * TILE, TILE)
                ids = (places(0) + start).astype(jnp.int16)
                total = jnp.where(named[0] == ids, one, none)
                for which in range(1, hashes):
                    total = total + jnp.where(named[which] == ids, one, none)
                slots_ref[pl.ds(start, TILE), span] = total.astype(F8)
            return carry

        lax.fori_loop(0, slots_ref.shape[0] // rows, step, 0)
        copies.append(
            pltpu.make_async_copy(slots_ref.at[:, span], slots_far.at[:, span], sem.at[part])
        )
        copies[-1].start()
    for copy in copies:
        copy.wait()


def forward_kernel(
    rows_ref, slots_ref, edges_ref, degree_ref, one_ref, two_ref, first_ref, second_ref,
    keys_a_ref, keys_b_ref, raw_ref, hidden_ref, inner_ref, slope_ref, wide_slots_ref, wide_edges_ref,
):
    seeds = SEED_DEV
    width = rows_ref.shape[1]
    slots = slots_ref[...].astype(BF16)
    wide_slots_ref[...] = slots
    features = split(tn(rows_ref[...], slots))
    for view in range(2):
        edges = edges_ref[view].astype(BF16)
        wide_edges_ref[view] = edges
        degree = degree_ref[view : view + 1, :]
        summed = nn(features, edges)
        layer_in = ((summed[:width] + summed[width:]) / degree).astype(BF16)
        hidden = jnp.maximum(tn(one_ref[...], layer_in), 0.0).astype(BF16)
        hidden_ref[view] = hidden
        seed_in = (nn(hidden, edges[:, :seeds]) / degree[:, :seeds]).astype(BF16)
        inner = jnp.maximum(tn(two_ref[...], seed_in), 0.0).astype(BF16)
        before = tn(first_ref[...], inner)
        grown = jnp.exp(jnp.minimum(before, 0.0))
        near_zero = before * (1.0 + before * (0.5 + before * (1.0 / 6.0)))
        below = jnp.where(before > -0.01, near_zero, grown - 1.0)
        projected = jnp.where(before > 0.0, before, below).astype(BF16)
        raw = tn(second_ref[...], projected)
        scale = lax.rsqrt(jnp.sum(raw * raw, axis=0, keepdims=True) + EPSILON)
        span = slice(view * seeds, (view + 1) * seeds)
        (keys_a_ref, keys_b_ref)[view][...] = (raw * scale).astype(BF16)
        raw_ref[:, span] = raw
        inner_ref[:, span] = inner
        slope_ref[:, span] = jnp.where(before > 0.0, 1.0, grown)


def flip(row):
    return jnp.broadcast_to(row, (128, row.shape[1])).T[:, :1]


def pair_expo(left, right_t, same=None):
    expo = jnp.exp(nn(left, right_t) * (1.0 / TEMPER))
    return expo if same is None else jnp.where(same, 0.0, expo)


def diagonal(count):
    down = lax.broadcasted_iota(jnp.int32, (count, count), 0)
    return down == lax.broadcasted_iota(jnp.int32, (count, count), 1)


def down_sum(expo):
    return jnp.sum(expo, axis=0, keepdims=True)


def across_sum(expo):
    return jnp.sum(expo, axis=1, keepdims=True)


def joined(refs):
    return jnp.concatenate([ref[...] for ref in refs], axis=1)


def early_kernel(
    key0a_ref, key0b_ref, key1a_ref, key1b_ref, key3a_ref, key3b_ref,
    expo_ref, total0_ref, totals_ref,
):
    own = joined((key0a_ref, key0b_ref))
    ahead = joined((key1a_ref, key1b_ref))
    behind = joined((key3a_ref, key3b_ref))
    count = own.shape[1]
    same = diagonal(count)
    expo = pair_expo(own.T, own, same)
    expo_ref[:count, :] = expo
    total0 = down_sum(expo)
    left = ahead.T
    expo = pair_expo(left, own)
    expo_ref[count : 2 * count, :] = expo
    total0 = total0 + down_sum(expo)
    total1 = across_sum(expo) + across_sum(pair_expo(left, ahead, same))
    left = behind.T
    expo = pair_expo(left, own)
    expo_ref[2 * count :, :] = expo
    total0 = total0 + down_sum(expo)
    total3 = across_sum(expo) + across_sum(pair_expo(left, behind, same))
    expo = pair_expo(left, ahead)
    total3 = total3 + across_sum(expo)
    total1 = total1 + flip(down_sum(expo))
    total0_ref[...] = total0
    totals_ref[:count, :] = total1
    totals_ref[count:, :] = total3


def backward_kernel(
    key0a_ref, key0b_ref, key1a_ref, key1b_ref, key3a_ref, key3b_ref, key2a_ref, key2b_ref,
    expo_ref, total0_ref, totals_ref,
    raw_ref, hidden_ref, inner_ref, slope_ref,
    slots_ref, edges_ref, degree_ref, one_ref, two_ref, first_ref, second_ref,
    grads_ref,
):
    seeds = SEED_DEV
    own = joined((key0a_ref, key0b_ref))
    ahead = joined((key1a_ref, key1b_ref))
    behind = joined((key3a_ref, key3b_ref))
    far = joined((key2a_ref, key2b_ref))
    count = far.shape[1]
    left = far.T
    last = pair_expo(left, own)
    total0 = total0_ref[...] + down_sum(last)
    total2 = across_sum(last) + across_sum(pair_expo(left, far, diagonal(count)))
    expo = pair_expo(left, ahead)
    total2 = total2 + across_sum(expo)
    total1 = totals_ref[:count, :] + flip(down_sum(expo))
    expo = pair_expo(left, behind)
    total2 = total2 + across_sum(expo)
    total3 = totals_ref[count:, :] + flip(down_sum(expo))
    own_inverse = 1.0 / total0
    pulled = jnp.zeros(far.shape, F32)
    blocks = (
        (own, expo_ref[:count, :], flip(total0)),
        (ahead, expo_ref[count : 2 * count, :], total1),
        (behind, expo_ref[2 * count :, :], total3),
        (far, last, total2),
    )
    for block, expo, total in blocks:
        weights = (expo * (own_inverse + 1.0 / total)).astype(BF16)
        pulled = pulled + nn(block, weights)
    feature_grads = None
    for view in range(2):
        span = slice(view * seeds, (view + 1) * seeds)
        partner = (key0b_ref, key0a_ref)[view][...].astype(F32)
        key_grads = (pulled[:, span] - 2.0 * partner) * (1.0 / TEMPER)
        raw = raw_ref[:, span]
        scale = lax.rsqrt(jnp.sum(raw * raw, axis=0, keepdims=True) + EPSILON)
        along = jnp.sum(raw * key_grads, axis=0, keepdims=True) * (scale * scale)
        raw_grads = ((key_grads - raw * along) * scale).astype(BF16)
        grads = nn(second_ref[...], raw_grads).astype(BF16).astype(F32)
        grads = (grads * slope_ref[:, span]).astype(BF16)
        grads = nn(first_ref[...], grads).astype(BF16)
        grads = jnp.where(inner_ref[:, span] > 0, grads, jnp.zeros_like(grads))
        grads = nn(two_ref[...], grads).astype(BF16).astype(F32)
        degree = degree_ref[view : view + 1, :]
        wide = grads.shape[0]
        grads = nt(split(grads / degree[:, :seeds]), edges_ref[view, :, :seeds])
        grads = (grads[:wide] + grads[wide:]).astype(BF16)
        grads = jnp.where(hidden_ref[view] > 0, grads, jnp.zeros_like(grads))
        grads = nn(one_ref[...], grads).astype(BF16).astype(F32)
        grads = nt(split(grads / degree), edges_ref[view])
        feature_grads = grads if feature_grads is None else feature_grads + grads
    width = feature_grads.shape[0] // 2
    feature_grads = split(feature_grads[:width] + feature_grads[width:])
    slot_grads = nt(slots_ref[...], feature_grads)
    grads_ref[...] = (slot_grads[:, :width] + slot_grads[:, width:]).astype(BF16)


def slabs_kernel(flat_ref, out_ref):
    slabs, slots = out_ref.shape
    for slab in range(slabs):
        out_ref[slab : slab + 1, :] = flat_ref[:, slab * slots : (slab + 1) * slots]


def fetch_kernel(
    asked_ref, table_ref, out_ref, again_ref, wide_ref, rows_ref, row_ref, index_ref, sem
):
    slabs, slots = index_ref.shape
    asked = asked_ref[...]
    row_ref[...] = jnp.maximum(asked, 0)
    copy = pltpu.make_async_copy(row_ref, index_ref, sem)
    copy.start()
    again_ref[...] = asked
    wide_ref[...] = table_ref[...].astype(F32)
    copy.wait()

    def step(pair, carry):
        for which in range(2):
            slab = 2 * pair + which
            start = pl.multiple_of(slab * slots, slots)
            for slot in range(slots):
                row = index_ref[slab, slot]
                rows_ref[pl.ds(start + slot, 1), :] = wide_ref[pl.ds(row, 1), :]
        return carry

    lax.fori_loop(0, slabs // 2, step, 0)
    out_ref[...] = rows_ref[...].astype(BF16).reshape(out_ref.shape)


def scatter_kernel(*refs, spans, first):
    out_ref = refs[-1]
    parts = 4
    rows = out_ref.shape[0] // parts
    picks, pieces = [], []
    for place, span in enumerate(spans):
        row_ref, lane_ref, grads_ref = refs[3 * place : 3 * place + 3]
        low = row_ref[:, span] & (rows - 1)
        hit = low == lax.broadcasted_iota(jnp.int32, (rows, low.shape[1]), 0)
        pick = jnp.where(hit, 1.0, 0.0).astype(BF16)
        grads = grads_ref[...]
        part_of = lane_ref[span, :]
        zero = jnp.zeros_like(grads)
        chosen = [jnp.where(part_of == part, grads, zero) for part in range(parts)]
        picks.append(pick)
        pieces.append(jnp.concatenate(chosen, axis=1))
    added = sum(nn(pick, chosen) for pick, chosen in zip(picks, pieces))
    width = out_ref.shape[1]
    for part in range(parts):
        span = slice(part * rows, (part + 1) * rows)
        value = added[:, part * width : (part + 1) * width]
        out_ref[span, :] = value if first else value + refs[-2][span, :]


def body(
    embedding_table,
    request_rows,
    node_slots,
    neighbours,
    kept_edges,
    weight_one,
    weight_two,
    proj_first,
    proj_second,
):
    table_count = lax.axis_size("table")
    batch_count = lax.axis_size("batch")
    shard_rows, width = embedding_table.shape
    nodes = neighbours.shape[0]
    seeds = SEED_DEV
    slot_count = request_rows.size
    (requests,) = call(
        slabs_kernel,
        [jax.ShapeDtypeStruct((table_count, slot_count // table_count), jnp.int32)],
        [request_rows],
        flops=1000,
        moved=50_000,
        mib=2,
    )

    def turn(value, by):
        return lax.ppermute(
            value, "batch", [(source, (source + by) % batch_count) for source in range(batch_count)]
        )

    received = lax.all_to_all(requests, "table", split_axis=0, concat_axis=0, tiled=True)
    (slots,) = call(
        slots_kernel,
        [jax.ShapeDtypeStruct((slot_count, nodes), F8)],
        [node_slots.T],
        flops=10_000_000,
        moved=2 * nodes * slot_count,
        mib=60,
        scratch=[
            pltpu.VMEM((slot_count, nodes), F8),
            pltpu.SemaphoreType.DMA((nodes // LANES,)),
        ],
        far_outs=(0,),
    )
    fetched, received = call(
        fetch_kernel,
        [
            jax.ShapeDtypeStruct(requests.shape + (width,), BF16),
            jax.ShapeDtypeStruct(requests.shape, jnp.int32),
        ],
        [received, embedding_table],
        flops=1_000_000,
        moved=6_000_000,
        mib=24,
        scratch=[
            pltpu.VMEM((shard_rows, width), F32),
            pltpu.VMEM((slot_count, width), F32),
            pltpu.VMEM(requests.shape, jnp.int32),
            pltpu.SMEM(requests.shape, jnp.int32),
            pltpu.SemaphoreType.DMA,
        ],
    )
    arrived = lax.all_to_all(fetched, "table", split_axis=0, concat_axis=0, tiled=True)

    fetched, received, near, kept = lax.optimization_barrier(
        (fetched, received, neighbours.T, kept_edges)
    )
    kept = kept.transpose(0, 2, 1).astype(F32)
    degree = 1.0 + jnp.sum(kept, axis=1)
    (edges,) = call(
        edges_kernel,
        [jax.ShapeDtypeStruct((2, nodes, nodes), F8)],
        [near, kept],
        flops=60_000_000,
        moved=4 * nodes * nodes,
        mib=60,
        scratch=[
            pltpu.VMEM((2, nodes, nodes), F8),
            pltpu.SemaphoreType.DMA((nodes // LANES,)),
        ],
        far_outs=(0,),
    )
    out_rows = shard_rows // batch_count
    part_rows = out_rows // 4
    offset = lax.axis_index("batch") * out_rows
    owned = []
    for by in range(batch_count):
        index = (received if by == 0 else turn(received, by)).reshape(-1) - offset
        part_of = jnp.where(index < 0, -1, index // part_rows).astype(BF16)
        owned.append((index[None, :], part_of))
    arrived, owned, edges, slots, degree = lax.optimization_barrier(
        (arrived, owned, edges, slots, degree)
    )
    rows = arrived.reshape(slot_count, width)

    wide = weight_one.shape[1]
    keys_a, keys_b, raw, hidden, inner, slope, slots, edges = call(
        forward_kernel,
        [
            jax.ShapeDtypeStruct((wide, seeds), BF16),
            jax.ShapeDtypeStruct((wide, seeds), BF16),
            jax.ShapeDtypeStruct((wide, 2 * seeds), F32),
            jax.ShapeDtypeStruct((2, wide, nodes), BF16),
            jax.ShapeDtypeStruct((wide, 2 * seeds), BF16),
            jax.ShapeDtypeStruct((wide, 2 * seeds), F32),
            jax.ShapeDtypeStruct((slot_count, nodes), BF16),
            jax.ShapeDtypeStruct((2, nodes, nodes), BF16),
        ],
        [rows, slots, edges, degree, weight_one, weight_two, proj_first, proj_second],
        flops=2_400_000_000,
        moved=10_000_000,
        mib=32,
    )
    ahead_b, behind_a = turn(keys_b, 1), turn(keys_a, 3)
    ahead_a, behind_b = turn(keys_a, 1), turn(keys_b, 3)
    far_b, far_a = turn(ahead_b, 1), turn(behind_a, 3)
    expo, total0, totals = call(
        early_kernel,
        [
            jax.ShapeDtypeStruct((6 * seeds, 2 * seeds), F32),
            jax.ShapeDtypeStruct((1, 2 * seeds), F32),
            jax.ShapeDtypeStruct((4 * seeds, 1), F32),
        ],
        [keys_a, keys_b, ahead_a, ahead_b, behind_a, behind_b],
        flops=800_000_000,
        moved=4_000_000,
        mib=16,
    )
    (grads,) = call(
        backward_kernel,
        [jax.ShapeDtypeStruct((slot_count, width), BF16)],
        [
            keys_a, keys_b, ahead_a, ahead_b, behind_a, behind_b, far_a, far_b,
            expo, total0, totals, raw, hidden, inner, slope,
            slots, edges, degree, weight_one, weight_two, proj_first, proj_second,
        ],
        flops=8_000_000_000,
        moved=12_000_000,
        mib=32,
    )
    returned = lax.all_to_all(
        grads.reshape(table_count, -1, width), "table", split_axis=0, concat_axis=0, tiled=True
    ).reshape(slot_count, width)

    half = slot_count // 2
    upper, lower = slice(0, half), slice(half, slot_count)
    from_left = [turn(returned[upper], 1)]
    from_right = [turn(returned[lower], 3)]
    from_left[0], from_right[0], owned = lax.optimization_barrier(
        (from_left[0], from_right[0], owned)
    )
    owned = [
        (index, jnp.broadcast_to(part_of[:, None], (slot_count, width))) for index, part_of in owned
    ]
    from_left.append(turn(returned[lower], 1))
    owned[0], owned[2] = lax.optimization_barrier((owned[0], owned[2]))
    from_right.append(turn(returned[upper], 3))
    from_far = [turn(from_left[0], 1), turn(from_right[0], 3)]
    rounds = (
        ((0, slice(0, slot_count), returned),),
        ((1, upper, from_left[0]), (3, lower, from_right[0])),
        ((1, lower, from_left[1]), (3, upper, from_right[1])),
        ((2, upper, from_far[0]), (2, lower, from_far[1])),
    )
    total = None
    for pieces in rounds:
        args = []
        for source, span, piece in pieces:
            args += [*owned[source], piece]
        args += [] if total is None else [total]
        (total,) = call(
            functools.partial(
                scatter_kernel, spans=[span for _, span, _ in pieces], first=total is None
            ),
            [jax.ShapeDtypeStruct((out_rows, width), F32)],
            args,
            flops=1_000_000_000,
            moved=4_000_000,
            mib=16,
        )
    return total


def solution(mesh):
    in_specs = (
        P("table", None),
        P(("table", "batch"), None),
        P(("table", "batch"), None),
        P(("table", "batch"), None),
        P(None, ("table", "batch"), None),
        P(),
        P(),
        P(),
        P(),
    )
    out_specs = P(("table", "batch"), None)
    return jax.shard_map(body, mesh=mesh, in_specs=in_specs, out_specs=out_specs, check_vma=False)
```

```python
import functools

import jax
import jax.numpy as jnp
from jax import lax
from jax.experimental import pallas as pl
from jax.experimental.pallas import tpu as pltpu
from jax.sharding import PartitionSpec as P

SEED_DEV = 256
TEMPER = 0.25
EPSILON = 1e-06
F32 = jnp.float32
BF16 = jnp.bfloat16
F8 = jnp.float8_e4m3fn
VMEM = pl.BlockSpec(memory_space=pltpu.VMEM)
HBM = pl.BlockSpec(memory_space=pltpu.HBM)


def nn(left, right):
    return lax.dot_general(left, right, (((1,), (0,)), ((), ())), preferred_element_type=F32)


def nt(left, right):
    return lax.dot_general(left, right, (((1,), (1,)), ((), ())), preferred_element_type=F32)


def tn(left, right):
    return lax.dot_general(left, right, (((0,), (0,)), ((), ())), preferred_element_type=F32)


def split(values):
    high = values.astype(BF16)
    low = (values - high.astype(F32)).astype(BF16)
    return jnp.concatenate([high, low], axis=0)


def call(kernel, outs, args, flops, moved, mib, scratch=(), far=(), far_outs=()):
    return pl.pallas_call(
        kernel,
        out_shape=outs,
        in_specs=[
            HBM if place in far else VMEM for place in range(len(args))
        ],
        out_specs=[HBM if place in far_outs else VMEM for place in range(len(outs))],
        scratch_shapes=list(scratch),
        compiler_params=pltpu.CompilerParams(vmem_limit_bytes=mib * 1024 * 1024),
        cost_estimate=pl.CostEstimate(flops=flops, bytes_accessed=moved, transcendentals=0),
    )(*args)


TILE, LANES, ROWS = 32, 128, 256


def spread(row, kind):
    return jnp.broadcast_to(row, (TILE, LANES)).astype(kind)


def places(axis):
    return lax.broadcasted_iota(jnp.int32, (TILE, LANES), axis)


def edges_kernel(near_ref, kept_ref, edges_far, edges_ref, sem):
    views, degree, nodes = kept_ref.shape
    none = jnp.zeros((), BF16)
    copies = []
    for part in range(nodes // LANES):
        span = slice(part * LANES, (part + 1) * LANES)
        nears = [spread(near_ref[slot : slot + 1, span], jnp.int16) for slot in range(degree)]
        kept = [
            [spread(kept_ref[view, slot : slot + 1, span], BF16) for slot in range(degree)]
            for view in range(views)
        ]

        def step(block, carry):
            for tile in range(ROWS // TILE):
                start = pl.multiple_of(block * ROWS + tile * TILE, TILE)
                ids = places(0) + start
                own = jnp.where(ids == places(1) + part * LANES, 1.0, 0.0).astype(BF16)
                ids = ids.astype(jnp.int16)
                totals = [own] * views
                for slot in range(degree):
                    hit = nears[slot] == ids
                    for view in range(views):
                        totals[view] = totals[view] + jnp.where(hit, kept[view][slot], none)
                for view in range(views):
                    edges_ref[view, pl.ds(start, TILE), span] = totals[view].astype(F8)
            return carry

        lax.fori_loop(0, nodes // ROWS, step, 0)
        copies.append(
            pltpu.make_async_copy(edges_ref.at[:, :, span], edges_far.at[:, :, span], sem.at[part])
        )
        copies[-1].start()
    for copy in copies:
        copy.wait()


def slots_kernel(slot_ref, slots_far, slots_ref, sem):
    hashes, nodes = slot_ref.shape
    rows = min(512, slots_ref.shape[0])
    one, none = jnp.ones((), BF16), jnp.zeros((), BF16)
    copies = []
    for part in range(nodes // LANES):
        span = slice(part * LANES, (part + 1) * LANES)
        named = [spread(slot_ref[which : which + 1, span], jnp.int16) for which in range(hashes)]

        def step(block, carry):
            for tile in range(rows // TILE):
                start = pl.multiple_of(block * rows + tile * TILE, TILE)
                ids = (places(0) + start).astype(jnp.int16)
                total = jnp.where(named[0] == ids, one, none)
                for which in range(1, hashes):
                    total = total + jnp.where(named[which] == ids, one, none)
                slots_ref[pl.ds(start, TILE), span] = total.astype(F8)
            return carry

        lax.fori_loop(0, slots_ref.shape[0] // rows, step, 0)
        copies.append(
            pltpu.make_async_copy(slots_ref.at[:, span], slots_far.at[:, span], sem.at[part])
        )
        copies[-1].start()
    for copy in copies:
        copy.wait()


def forward_kernel(
    rows_ref, slots_ref, edges_ref, degree_ref, one_ref, two_ref, first_ref, second_ref,
    keys_a_ref, keys_b_ref, raw_ref, hidden_ref, inner_ref, slope_ref, wide_slots_ref, wide_edges_ref,
):
    seeds = SEED_DEV
    width = rows_ref.shape[1]
    slots = slots_ref[...].astype(BF16)
    wide_slots_ref[...] = slots
    features = split(tn(rows_ref[...], slots))
    for view in range(2):
        edges = edges_ref[view].astype(BF16)
        wide_edges_ref[view] = edges
        degree = degree_ref[view : view + 1, :]
        summed = nn(features, edges)
        layer_in = ((summed[:width] + summed[width:]) / degree).astype(BF16)
        hidden = jnp.maximum(tn(one_ref[...], layer_in), 0.0).astype(BF16)
        hidden_ref[view] = hidden
        seed_in = (nn(hidden, edges[:, :seeds]) / degree[:, :seeds]).astype(BF16)
        inner = jnp.maximum(tn(two_ref[...], seed_in), 0.0).astype(BF16)
        before = tn(first_ref[...], inner)
        grown = jnp.exp(jnp.minimum(before, 0.0))
        near_zero = before * (1.0 + before * (0.5 + before * (1.0 / 6.0)))
        below = jnp.where(before > -0.01, near_zero, grown - 1.0)
        projected = jnp.where(before > 0.0, before, below).astype(BF16)
        raw = tn(second_ref[...], projected)
        scale = lax.rsqrt(jnp.sum(raw * raw, axis=0, keepdims=True) + EPSILON)
        span = slice(view * seeds, (view + 1) * seeds)
        (keys_a_ref, keys_b_ref)[view][...] = (raw * scale).astype(BF16)
        raw_ref[:, span] = raw
        inner_ref[:, span] = inner
        slope_ref[:, span] = jnp.where(before > 0.0, 1.0, grown)


def flip(row):
    return jnp.broadcast_to(row, (128, row.shape[1])).T[:, :1]


def pair_expo(left, right_t, same=None):
    expo = jnp.exp(nn(left, right_t) * (1.0 / TEMPER))
    return expo if same is None else jnp.where(same, 0.0, expo)


def diagonal(count):
    down = lax.broadcasted_iota(jnp.int32, (count, count), 0)
    return down == lax.broadcasted_iota(jnp.int32, (count, count), 1)


def down_sum(expo):
    return jnp.sum(expo, axis=0, keepdims=True)


def across_sum(expo):
    return jnp.sum(expo, axis=1, keepdims=True)


def joined(refs):
    return jnp.concatenate([ref[...] for ref in refs], axis=1)


def early_kernel(
    key0a_ref, key0b_ref, key1a_ref, key1b_ref, key3a_ref, key3b_ref,
    expo_ref, total0_ref, totals_ref,
):
    own = joined((key0a_ref, key0b_ref))
    ahead = joined((key1a_ref, key1b_ref))
    behind = joined((key3a_ref, key3b_ref))
    count = own.shape[1]
    same = diagonal(count)
    expo = pair_expo(own.T, own, same)
    expo_ref[:count, :] = expo
    total0 = down_sum(expo)
    left = ahead.T
    expo = pair_expo(left, own)
    expo_ref[count : 2 * count, :] = expo
    total0 = total0 + down_sum(expo)
    total1 = across_sum(expo) + across_sum(pair_expo(left, ahead, same))
    left = behind.T
    expo = pair_expo(left, own)
    expo_ref[2 * count :, :] = expo
    total0 = total0 + down_sum(expo)
    total3 = across_sum(expo) + across_sum(pair_expo(left, behind, same))
    expo = pair_expo(left, ahead)
    total3 = total3 + across_sum(expo)
    total1 = total1 + flip(down_sum(expo))
    total0_ref[...] = total0
    totals_ref[:count, :] = total1
    totals_ref[count:, :] = total3


def backward_kernel(
    key0a_ref, key0b_ref, key1a_ref, key1b_ref, key3a_ref, key3b_ref, key2a_ref, key2b_ref,
    expo_ref, total0_ref, totals_ref,
    raw_ref, hidden_ref, inner_ref, slope_ref,
    slots_ref, edges_ref, degree_ref, one_ref, two_ref, first_ref, second_ref,
    grads_ref,
):
    seeds = SEED_DEV
    own = joined((key0a_ref, key0b_ref))
    ahead = joined((key1a_ref, key1b_ref))
    behind = joined((key3a_ref, key3b_ref))
    far = joined((key2a_ref, key2b_ref))
    count = far.shape[1]
    left = far.T
    last = pair_expo(left, own)
    total0 = total0_ref[...] + down_sum(last)
    total2 = across_sum(last) + across_sum(pair_expo(left, far, diagonal(count)))
    expo = pair_expo(left, ahead)
    total2 = total2 + across_sum(expo)
    total1 = totals_ref[:count, :] + flip(down_sum(expo))
    expo = pair_expo(left, behind)
    total2 = total2 + across_sum(expo)
    total3 = totals_ref[count:, :] + flip(down_sum(expo))
    own_inverse = 1.0 / total0
    pulled = jnp.zeros(far.shape, F32)
    blocks = (
        (own, expo_ref[:count, :], flip(total0)),
        (ahead, expo_ref[count : 2 * count, :], total1),
        (behind, expo_ref[2 * count :, :], total3),
        (far, last, total2),
    )
    for block, expo, total in blocks:
        weights = (expo * (own_inverse + 1.0 / total)).astype(BF16)
        pulled = pulled + nn(block, weights)
    feature_grads = None
    for view in range(2):
        span = slice(view * seeds, (view + 1) * seeds)
        partner = (key0b_ref, key0a_ref)[view][...].astype(F32)
        key_grads = (pulled[:, span] - 2.0 * partner) * (1.0 / TEMPER)
        raw = raw_ref[:, span]
        scale = lax.rsqrt(jnp.sum(raw * raw, axis=0, keepdims=True) + EPSILON)
        along = jnp.sum(raw * key_grads, axis=0, keepdims=True) * (scale * scale)
        raw_grads = ((key_grads - raw * along) * scale).astype(BF16)
        grads = nn(second_ref[...], raw_grads).astype(BF16).astype(F32)
        grads = (grads * slope_ref[:, span]).astype(BF16)
        grads = nn(first_ref[...], grads).astype(BF16)
        grads = jnp.where(inner_ref[:, span] > 0, grads, jnp.zeros_like(grads))
        grads = nn(two_ref[...], grads).astype(BF16).astype(F32)
        degree = degree_ref[view : view + 1, :]
        wide = grads.shape[0]
        grads = nt(split(grads / degree[:, :seeds]), edges_ref[view, :, :seeds])
        grads = (grads[:wide] + grads[wide:]).astype(BF16)
        grads = jnp.where(hidden_ref[view] > 0, grads, jnp.zeros_like(grads))
        grads = nn(one_ref[...], grads).astype(BF16).astype(F32)
        grads = nt(split(grads / degree), edges_ref[view])
        feature_grads = grads if feature_grads is None else feature_grads + grads
    width = feature_grads.shape[0] // 2
    feature_grads = split(feature_grads[:width] + feature_grads[width:])
    slot_grads = nt(slots_ref[...], feature_grads)
    grads_ref[...] = (slot_grads[:, :width] + slot_grads[:, width:]).astype(BF16)


def slabs_kernel(flat_ref, out_ref):
    slabs, slots = out_ref.shape
    for slab in range(slabs):
        out_ref[slab : slab + 1, :] = flat_ref[:, slab * slots : (slab + 1) * slots]


def fetch_kernel(
    asked_ref, table_ref, out_ref, again_ref, wide_ref, rows_ref, row_ref, index_ref, sem
):
    slabs, slots = index_ref.shape
    asked = asked_ref[...]
    row_ref[...] = jnp.maximum(asked, 0)
    copy = pltpu.make_async_copy(row_ref, index_ref, sem)
    copy.start()
    again_ref[...] = asked
    wide_ref[...] = table_ref[...].astype(F32)
    copy.wait()

    def step(pair, carry):
        for which in range(2):
            slab = 2 * pair + which
            start = pl.multiple_of(slab * slots, slots)
            for slot in range(slots):
                row = index_ref[slab, slot]
                rows_ref[pl.ds(start + slot, 1), :] = wide_ref[pl.ds(row, 1), :]
        return carry

    lax.fori_loop(0, slabs // 2, step, 0)
    out_ref[...] = rows_ref[...].astype(BF16).reshape(out_ref.shape)


def scatter_kernel(*refs, spans, first):
    out_ref = refs[-1]
    parts = 4
    rows = out_ref.shape[0] // parts
    picks, pieces = [], []
    for place, span in enumerate(spans):
        row_ref, lane_ref, grads_ref = refs[3 * place : 3 * place + 3]
        low = row_ref[:, span] & (rows - 1)
        hit = low == lax.broadcasted_iota(jnp.int32, (rows, low.shape[1]), 0)
        pick = jnp.where(hit, 1.0, 0.0).astype(BF16)
        grads = grads_ref[...]
        part_of = lane_ref[span, :]
        zero = jnp.zeros_like(grads)
        chosen = [jnp.where(part_of == part, grads, zero) for part in range(parts)]
        picks.append(pick)
        pieces.append(jnp.concatenate(chosen, axis=1))
    added = sum(nn(pick, chosen) for pick, chosen in zip(picks, pieces))
    width = out_ref.shape[1]
    for part in range(parts):
        span = slice(part * rows, (part + 1) * rows)
        value = added[:, part * width : (part + 1) * width]
        out_ref[span, :] = value if first else value + refs[-2][span, :]


def body(
    embedding_table,
    request_rows,
    node_slots,
    neighbours,
    kept_edges,
    weight_one,
    weight_two,
    proj_first,
    proj_second,
):
    table_count = lax.axis_size("table")
    batch_count = lax.axis_size("batch")
    shard_rows, width = embedding_table.shape
    nodes = neighbours.shape[0]
    seeds = SEED_DEV
    slot_count = request_rows.size
    (requests,) = call(
        slabs_kernel,
        [jax.ShapeDtypeStruct((table_count, slot_count // table_count), jnp.int32)],
        [request_rows],
        flops=1000,
        moved=50_000,
        mib=2,
    )

    def turn(value, by):
        return lax.ppermute(
            value, "batch", [(source, (source + by) % batch_count) for source in range(batch_count)]
        )

    received = lax.all_to_all(requests, "table", split_axis=0, concat_axis=0, tiled=True)
    (slots,) = call(
        slots_kernel,
        [jax.ShapeDtypeStruct((slot_count, nodes), F8)],
        [node_slots.T],
        flops=10_000_000,
        moved=2 * nodes * slot_count,
        mib=60,
        scratch=[
            pltpu.VMEM((slot_count, nodes), F8),
            pltpu.SemaphoreType.DMA((nodes // LANES,)),
        ],
        far_outs=(0,),
    )
    fetched, received = call(
        fetch_kernel,
        [
            jax.ShapeDtypeStruct(requests.shape + (width,), BF16),
            jax.ShapeDtypeStruct(requests.shape, jnp.int32),
        ],
        [received, embedding_table],
        flops=1_000_000,
        moved=6_000_000,
        mib=24,
        scratch=[
            pltpu.VMEM((shard_rows, width), F32),
            pltpu.VMEM((slot_count, width), F32),
            pltpu.VMEM(requests.shape, jnp.int32),
            pltpu.SMEM(requests.shape, jnp.int32),
            pltpu.SemaphoreType.DMA,
        ],
    )
    arrived = lax.all_to_all(fetched, "table", split_axis=0, concat_axis=0, tiled=True)

    fetched, received, near, kept = lax.optimization_barrier(
        (fetched, received, neighbours.T, kept_edges)
    )
    kept = kept.transpose(0, 2, 1).astype(F32)
    degree = 1.0 + jnp.sum(kept, axis=1)
    (edges,) = call(
        edges_kernel,
        [jax.ShapeDtypeStruct((2, nodes, nodes), F8)],
        [near, kept],
        flops=60_000_000,
        moved=4 * nodes * nodes,
        mib=60,
        scratch=[
            pltpu.VMEM((2, nodes, nodes), F8),
            pltpu.SemaphoreType.DMA((nodes // LANES,)),
        ],
        far_outs=(0,),
    )
    out_rows = shard_rows // batch_count
    part_rows = out_rows // 4
    offset = lax.axis_index("batch") * out_rows
    owned = []
    for by in range(batch_count):
        index = (received if by == 0 else turn(received, by)).reshape(-1) - offset
        part_of = jnp.where(index < 0, -1, index // part_rows).astype(BF16)
        owned.append((index[None, :], part_of))
    arrived, owned, edges, slots, degree = lax.optimization_barrier(
        (arrived, owned, edges, slots, degree)
    )
    rows = arrived.reshape(slot_count, width)

    wide = weight_one.shape[1]
    keys_a, keys_b, raw, hidden, inner, slope, slots, edges = call(
        forward_kernel,
        [
            jax.ShapeDtypeStruct((wide, seeds), BF16),
            jax.ShapeDtypeStruct((wide, seeds), BF16),
            jax.ShapeDtypeStruct((wide, 2 * seeds), F32),
            jax.ShapeDtypeStruct((2, wide, nodes), BF16),
            jax.ShapeDtypeStruct((wide, 2 * seeds), BF16),
            jax.ShapeDtypeStruct((wide, 2 * seeds), F32),
            jax.ShapeDtypeStruct((slot_count, nodes), BF16),
            jax.ShapeDtypeStruct((2, nodes, nodes), BF16),
        ],
        [rows, slots, edges, degree, weight_one, weight_two, proj_first, proj_second],
        flops=2_400_000_000,
        moved=10_000_000,
        mib=32,
    )
    ahead_b, behind_a = turn(keys_b, 1), turn(keys_a, 3)
    ahead_a, behind_b = turn(keys_a, 1), turn(keys_b, 3)
    far_b, far_a = turn(ahead_b, 1), turn(behind_a, 3)
    expo, total0, totals = call(
        early_kernel,
        [
            jax.ShapeDtypeStruct((6 * seeds, 2 * seeds), F32),
            jax.ShapeDtypeStruct((1, 2 * seeds), F32),
            jax.ShapeDtypeStruct((4 * seeds, 1), F32),
        ],
        [keys_a, keys_b, ahead_a, ahead_b, behind_a, behind_b],
        flops=800_000_000,
        moved=4_000_000,
        mib=16,
    )
    (grads,) = call(
        backward_kernel,
        [jax.ShapeDtypeStruct((slot_count, width), BF16)],
        [
            keys_a, keys_b, ahead_a, ahead_b, behind_a, behind_b, far_a, far_b,
            expo, total0, totals, raw, hidden, inner, slope,
            slots, edges, degree, weight_one, weight_two, proj_first, proj_second,
        ],
        flops=8_000_000_000,
        moved=12_000_000,
        mib=32,
    )
    returned = lax.all_to_all(
        grads.reshape(table_count, -1, width), "table", split_axis=0, concat_axis=0, tiled=True
    ).reshape(slot_count, width)

    half = slot_count // 2
    upper, lower = slice(0, half), slice(half, slot_count)
    from_left = [turn(returned[upper], 1)]
    from_right = [turn(returned[lower], 3)]
    from_left[0], from_right[0], owned = lax.optimization_barrier(
        (from_left[0], from_right[0], owned)
    )
    owned = [
        (index, jnp.broadcast_to(part_of[:, None], (slot_count, width))) for index, part_of in owned
    ]
    from_left.append(turn(returned[lower], 1))
    owned[0], owned[2] = lax.optimization_barrier((owned[0], owned[2]))
    from_right.append(turn(returned[upper], 3))
    from_far = [turn(from_left[0], 1), turn(from_right[0], 3)]
    rounds = (
        ((0, slice(0, slot_count), returned),),
        ((1, upper, from_left[0]), (3, lower, from_right[0])),
        ((1, lower, from_left[1]), (3, upper, from_right[1])),
        ((2, upper, from_far[0]),),
        ((2, lower, from_far[1]),),
    )
    total = None
    for pieces in rounds:
        args = []
        for source, span, piece in pieces:
            args += [*owned[source], piece]
        args += [] if total is None else [total]
        (total,) = call(
            functools.partial(
                scatter_kernel, spans=[span for _, span, _ in pieces], first=total is None
            ),
            [jax.ShapeDtypeStruct((out_rows, width), F32)],
            args,
            flops=1_000_000_000,
            moved=4_000_000,
            mib=16,
        )
    return total


def solution(mesh):
    in_specs = (
        P("table", None),
        P(("table", "batch"), None),
        P(("table", "batch"), None),
        P(("table", "batch"), None),
        P(None, ("table", "batch"), None),
        P(),
        P(),
        P(),
        P(),
    )
    out_specs = P(("table", "batch"), None)
    return jax.shard_map(body, mesh=mesh, in_specs=in_specs, out_specs=out_specs, check_vma=False)
```
